32 devices in a mesh: dp: 8 (over y, x, core), tensor: 4 (over z).
Axes of the slice: x: 2, y: 2, z: 4, core: 2. Of those that a mesh axis runs over, the one named last changes fastest.
Arguments:
- base_codes: int32 [4096, 14336], P('dp', 'tensor'), may hold values from 0 to 15
- block_scales: float32 [4096, 224], P('dp', 'tensor'), may hold values from 0.0008 to 0.0176, as said below
- input_adapter_factor: bfloat16 [4096, 64], replicated, may hold values from -0.09375 to 0.09375
- output_adapter_factor: bfloat16 [64, 14336], P(None, 'tensor'), may hold values from -0.046875 to 0.046875
- magnitude: float32 [14336], P('tensor'), may hold values from 0.5 to 2
- inputs: bfloat16 [1536, 4096], P('dp', 'tensor'), may hold values from -6 to 6
- grad_out: bfloat16 [1536, 14336], P('dp', 'tensor'), may hold values from -1.5 to 1.5
- pre_scale: bfloat16 [1536, 14336], P('dp', 'tensor'), may hold values from -6 to 6
Outputs:
- grad_inputs: bfloat16 [1536, 4096], P('dp', 'tensor')
- input_adapter_gradient: float32 [4096, 64], P('tensor')
- output_adapter_gradient: float32 [64, 14336], P(None, 'tensor')
- grad_magnitude: float32 [14336], P('tensor')
The draws below stay inside these ranges and needn't reach their ends.
Inputs may be any that keep to these rules, and one draw needn't show every extreme that they name: `block_scales`: block scales of the 4-bit codes.
All inputs are finite; a program needn't handle non-finite values.
Results may differ from the reference program's by a relative error of at most 0.015.
Values may be sent and summed in bfloat16 or wider, within the bound.
A program may use at most 192 MiB of HBM per device.

```python
import math
import jax
import jax.numpy as jnp
from jax import lax

D = 4096
FF = 14336
R = 64
QBLOCK = 64
TOKENS = 1536
N_TENSOR = 4


def draw_block_scales(key, part):
    key = jax.random.fold_in(key, 7)
    grid_shape = (D, FF // QBLOCK)
    position = jnp.arange(D, dtype=jnp.float32) / D
    values = jnp.exp(jax.random.uniform(key, grid_shape, jnp.float32, math.log(0.0008), math.log(0.008)))
    row_ramp = 1.0 + 0.75 * position
    return values * row_ramp[:, None]


def touch_ends(values, key, low, top_value):
    longest = values.shape.index(max(values.shape))
    spots = []
    for shift in (0, 1):
        where = [jax.random.randint(jax.random.fold_in(key, axis), (), 0, length) for axis, length in enumerate(values.shape)]
        where[longest] = (where[longest] + shift) % values.shape[longest]
        spots.append(tuple(where))
    return values.at[spots[0]].set(low).at[spots[1]].set(top_value)


def block_scale(stream_key, shape, split, smallest, top_value):
    level = 1.0
    for dim, shards_of in split:
        heights = jax.random.uniform(jax.random.fold_in(jax.random.fold_in(stream_key, 6), dim), (shards_of,), jnp.float32, smallest / len(split), top_value / len(split))
        level = level * jnp.repeat(jnp.exp(heights), shape[dim] // shards_of).reshape((-1,) + (1,) * (len(shape) - 1 - dim))
    return level


def noise(own_key, shape, deviation, limit, shards=(), kind=jnp.bfloat16):
    array = jax.random.normal(own_key, shape, jnp.float32) * deviation
    if len(shards) > 0:
        array = block_scale(own_key, shape, shards, -0.22, 0.18) * array
    return jnp.clip(array, min=-limit, max=limit).astype(kind)


def setup_inputs(seed: int = 0) -> dict:
    arg_keys = jax.random.split(jax.random.key(seed), 9)
    return {
        "base_codes": touch_ends(jax.random.randint(arg_keys[0], (D, FF), 0, 16), jax.random.fold_in(arg_keys[0], 1), 0, 15).astype(jnp.int32),
        "block_scales": draw_block_scales(jax.random.fold_in(arg_keys[8], 71), 0),
        "input_adapter_factor": noise(arg_keys[2], (D, R), D ** -0.5, 0.09375),
        "output_adapter_factor": noise(arg_keys[3], (R, FF), FF ** -0.5, 0.046875, ((1, 4),)),
        "magnitude": jnp.clip(jnp.exp(math.log(2.0) - 1.3862944 * jax.random.uniform(arg_keys[4], (FF,), jnp.float32) ** block_scale(arg_keys[4], (FF,), ((0, 4),), -0.2, 0.2)), 0.5, 2.0),
        "inputs": noise(arg_keys[5], (TOKENS, D), 1.0, 6.0, ((0, 8), (1, 4))),
        "grad_out": noise(arg_keys[6], (TOKENS, FF), 0.25, 1.5, ((0, 8), (1, 4))),
        "pre_scale": noise(arg_keys[7], (TOKENS, FF), 1.0, 6.0, ((0, 8), (1, 4))),
    }


adapter_scale_factor = 0.5

def dequantize(base_codes, block_scales, block_size):
    expanded = jnp.repeat(block_scales, block_size, axis=1)
    return (base_codes.astype(jnp.float32) - 7.5) * expanded

def reference(base_codes, block_scales, input_adapter_factor, output_adapter_factor, magnitude, inputs, grad_out, pre_scale):
    dequantized_weight = dequantize(base_codes, block_scales, QBLOCK)
    merged_weight_matrix = (dequantized_weight + adapter_scale_factor * jnp.dot(input_adapter_factor, output_adapter_factor, preferred_element_type=jnp.float32)).astype(jnp.bfloat16)
    merged_f = lax.optimization_barrier(merged_weight_matrix).astype(jnp.float32)
    col_norm = jnp.sqrt(lax.optimization_barrier(jnp.sum(merged_f * merged_f, axis=0)) + 1e-06)
    grad_f = grad_out.astype(jnp.float32)
    scaled_weight_matrix = (grad_f * (magnitude / col_norm)).astype(jnp.bfloat16)
    quarter = FF // N_TENSOR
    summed = jnp.zeros((inputs.shape[0], D), jnp.float32)
    for tensor_index in range(N_TENSOR):
        lower = tensor_index * quarter
        block_sum = jnp.dot(scaled_weight_matrix[:, lower:lower + quarter], merged_weight_matrix[:, lower:lower + quarter].T, preferred_element_type=jnp.float32)
        rounded = lax.optimization_barrier(block_sum.astype(jnp.bfloat16))
        summed = summed + rounded.astype(jnp.float32)
    grad_inputs = summed.astype(jnp.bfloat16)
    hidden_lowrank_term = jnp.dot(inputs, input_adapter_factor, preferred_element_type=jnp.float32).astype(jnp.bfloat16)
    backward_lowrank_term = jnp.dot(scaled_weight_matrix, output_adapter_factor.T, preferred_element_type=jnp.float32).astype(jnp.bfloat16)
    input_adapter_gradient = adapter_scale_factor * jnp.dot(inputs.T, backward_lowrank_term, preferred_element_type=jnp.float32)
    output_adapter_gradient = adapter_scale_factor * jnp.dot(hidden_lowrank_term.T, scaled_weight_matrix, preferred_element_type=jnp.float32)
    grad_magnitude = lax.optimization_barrier(jnp.sum(grad_f * pre_scale.astype(jnp.float32), axis=0)) / col_norm
    return (grad_inputs, input_adapter_gradient, output_adapter_gradient, grad_magnitude)
```

```python
import jax
import jax.numpy as jnp
from jax import lax
from jax.sharding import PartitionSpec as P

adapter_scale_factor = 0.5


def on_device(
    base_codes,
    block_scales,
    input_adapter_factor,
    output_adapter_factor,
    magnitude,
    inputs,
    grad_out,
    pre_scale,
):
    f32, bf16 = jnp.float32, jnp.bfloat16
    row_count, columns = base_codes.shape
    tokens = grad_out.shape[0]
    dp = lax.axis_index("dp")
    block_size = columns // block_scales.shape[1]
    gathered = lax.all_gather(grad_out, "dp", axis=0, tiled=True)
    quarter_d = inputs.shape[1]
    adapter_part = lax.dynamic_slice_in_dim(
        input_adapter_factor, lax.axis_index("tensor") * quarter_d, quarter_d, 0
    )
    hidden_low = lax.psum(
        jnp.dot(inputs, adapter_part, preferred_element_type=f32).astype(bf16), "tensor"
    )
    hidden_all = lax.all_gather(hidden_low, "dp", axis=0, tiled=True)
    expanded = jnp.repeat(block_scales, block_size, axis=1)
    adapter_row_block = lax.dynamic_slice_in_dim(
        input_adapter_factor, dp * row_count, row_count, 0
    )
    merged = (
        (base_codes.astype(f32) - 7.5) * expanded
        + adapter_scale_factor
        * jnp.dot(adapter_row_block, output_adapter_factor, preferred_element_type=f32)
    ).astype(bf16)
    merged_f = merged.astype(f32)
    column_sums = jnp.sum(merged_f * merged_f, axis=0)
    magnitude_sums = jnp.sum(grad_out.astype(f32) * pre_scale.astype(f32), axis=0)
    column_sums, magnitude_sums = lax.psum((column_sums, magnitude_sums), "dp")
    col_norm = jnp.sqrt(column_sums + 1e-06)
    scaled = (gathered.astype(f32) * (magnitude / col_norm)).astype(bf16)
    partial_value = jnp.einsum("tf,rf->tr", scaled, merged, preferred_element_type=f32)
    exchanged = lax.all_to_all(
        partial_value.astype(bf16), "dp", split_axis=0, concat_axis=1, tiled=True
    )
    grad_inputs = lax.psum_scatter(exchanged, "tensor", scatter_dimension=1, tiled=True)
    own_scaled = lax.dynamic_slice_in_dim(scaled, dp * tokens, tokens, 0)
    back_low = lax.psum(
        jnp.einsum(
            "tf,rf->tr", own_scaled, output_adapter_factor, preferred_element_type=f32
        ).astype(bf16),
        "tensor",
    )
    input_gradient = lax.psum(
        adapter_scale_factor
        * jnp.einsum("td,tr->dr", inputs, back_low, preferred_element_type=f32),
        "dp",
    )
    output_gradient = adapter_scale_factor * jnp.einsum(
        "tr,tf->rf", hidden_all, scaled, preferred_element_type=f32
    )
    return (grad_inputs, input_gradient, output_gradient, magnitude_sums / col_norm)


def solution(mesh):
    in_specs = (
        P("dp", "tensor"),
        P("dp", "tensor"),
        P(),
        P(None, "tensor"),
        P("tensor"),
        P("dp", "tensor"),
        P("dp", "tensor"),
        P("dp", "tensor"),
    )
    out_specs = (P("dp", "tensor"), P("tensor", None), P(None, "tensor"), P("tensor"))
    return jax.shard_map(
        on_device, mesh=mesh, in_specs=in_specs, out_specs=out_specs, check_vma=False
    )
```

```python
import jax
import jax.numpy as jnp
from jax import lax
from jax.experimental import pallas as pl
from jax.experimental.pallas import tpu as pltpu
from jax.sharding import PartitionSpec as P

adapter_scale_factor = 0.5


def on_device(
    base_codes,
    block_scales,
    input_adapter_factor,
    output_adapter_factor,
    magnitude,
    inputs,
    grad_out,
    pre_scale,
):
    f32, bf16 = jnp.float32, jnp.bfloat16
    row_count, columns = base_codes.shape
    tokens = grad_out.shape[0]
    dp = lax.axis_index("dp")
    block_size = columns // block_scales.shape[1]
    gathered = lax.all_gather(grad_out, "dp", axis=0, tiled=True)
    quarter_d = inputs.shape[1]
    adapter_part = lax.dynamic_slice_in_dim(
        input_adapter_factor, lax.axis_index("tensor") * quarter_d, quarter_d, 0
    )
    hidden_low = lax.psum(
        jnp.dot(inputs, adapter_part, preferred_element_type=f32).astype(bf16), "tensor"
    )
    hidden_all = lax.all_gather(hidden_low, "dp", axis=0, tiled=True)
    expanded = jnp.repeat(block_scales, block_size, axis=1)
    adapter_row_block = lax.dynamic_slice_in_dim(
        input_adapter_factor, dp * row_count, row_count, 0
    )
    merged = (
        (base_codes.astype(f32) - 7.5) * expanded
        + adapter_scale_factor
        * jnp.dot(adapter_row_block, output_adapter_factor, preferred_element_type=f32)
    ).astype(bf16)
    merged_f = merged.astype(f32)
    column_sums = jnp.sum(merged_f * merged_f, axis=0)
    magnitude_sums = jnp.sum(grad_out.astype(f32) * pre_scale.astype(f32), axis=0)
    column_sums, magnitude_sums = lax.psum((column_sums, magnitude_sums), "dp")
    col_norm = jnp.sqrt(column_sums + 1e-06)
    scaled = (gathered.astype(f32) * (magnitude / col_norm)).astype(bf16)
    partial_value = jnp.einsum("tf,rf->tr", scaled, merged, preferred_element_type=f32)
    exchanged = lax.all_to_all(
        partial_value.astype(bf16), "dp", split_axis=0, concat_axis=1, tiled=True
    )
    grad_inputs = lax.psum_scatter(exchanged, "tensor", scatter_dimension=1, tiled=True)
    own_scaled = lax.dynamic_slice_in_dim(scaled, dp * tokens, tokens, 0)
    back_low = lax.psum(
        jnp.einsum(
            "tf,rf->tr", own_scaled, output_adapter_factor, preferred_element_type=f32
        ).astype(bf16),
        "tensor",
    )
    input_gradient = lax.psum(
        adapter_scale_factor
        * jnp.einsum("td,tr->dr", inputs, back_low, preferred_element_type=f32),
        "dp",
    )
    output_gradient = adapter_scale_factor * jnp.einsum(
        "tr,tf->rf", hidden_all, scaled, preferred_element_type=f32
    )
    return (grad_inputs, input_gradient, output_gradient, magnitude_sums / col_norm)


MESH = pl.DeviceIdType.MESH
COLUMN_TILE = 512


def flip(bit, by):
    return bit + by - 2 * bit * by


def fused_kernel(
    codes_hbm,
    scales_ref,
    first_ref,
    second_ref,
    magnitude_ref,
    inputs_ref,
    grad_hbm,
    pre_hbm,
    out_ref,
    first_out,
    second_out,
    magnitude_out,
    codes,
    pre,
    tokens,
    weight,
    stats,
    factor,
    low_parts,
    low,
    back_parts,
    back_acc,
    acc,
    product,
    returned,
    across,
    second_parts,
    second_pair,
    first_split,
    first_recv,
    first_full,
    local_sem,
    send_sem,
    recv_sem,
):
    f32, bf16 = jnp.float32, jnp.bfloat16
    rows, width = codes.shape
    count = tokens.shape[1]
    half = count // 2
    tile = COLUMN_TILE
    steps = width // tile
    rank = low.shape[2]
    block = width // scales_ref.shape[1]
    dp, z = lax.axis_index("dp"), lax.axis_index("tensor")
    core = lax.rem(dp, 2)
    x = lax.rem(dp // 2, 2)
    y = dp // 4
    z_low, z_high = lax.rem(z, 2), z // 2

    def plane(offset):
        return (
            flip(y, offset // 4) * 4 + flip(x, (offset // 2) % 2) * 2 + flip(core, offset % 2)
        )

    def stack(offset):
        return flip(z_high, offset // 2) * 2 + flip(z_low, offset % 2)

    used = [0]
    sent = []

    def remote(source, target, to, start=True):
        index = used[0]
        used[0] += 1
        copy = pltpu.make_async_remote_copy(
            src_ref=source,
            dst_ref=target,
            send_sem=send_sem.at[index],
            recv_sem=recv_sem.at[index],
            device_id=to,
            device_id_type=MESH,
        )
        copy.start()
        sent.append(copy)
        return copy

    def arrival(source, target, copy_index, to):
        return pltpu.make_async_remote_copy(
            src_ref=source,
            dst_ref=target,
            send_sem=send_sem.at[copy_index],
            recv_sem=recv_sem.at[copy_index],
            device_id=to,
            device_id_type=MESH,
        )

    def peer(offset):
        return {"dp": plane(offset), "tensor": z}

    def over(offset):
        return {"dp": dp, "tensor": stack(offset)}

    codes_copy = pltpu.make_async_copy(codes_hbm, codes, local_sem.at[0])
    pre_copy = pltpu.make_async_copy(pre_hbm, pre, local_sem.at[1])
    own_copy = pltpu.make_async_copy(grad_hbm, tokens.at[0], local_sem.at[2])
    codes_copy.start()
    pre_copy.start()
    own_copy.start()

    barrier = pltpu.get_barrier_semaphore()
    for offset in range(1, 8):
        pl.semaphore_signal(barrier, inc=1, device_id=peer(offset), device_id_type=MESH)
    for offset in range(1, 4):
        pl.semaphore_signal(barrier, inc=1, device_id=over(offset), device_id_type=MESH)
    pl.semaphore_wait(barrier, 10)

    lower, upper = pl.ds(0, half), pl.ds(half, half)
    from_x = [
        remote(grad_hbm.at[lower], tokens.at[1, lower], peer(2)),
    ]
    from_y = [
        remote(grad_hbm.at[upper], tokens.at[2, upper], peer(4)),
    ]
    from_x.append(remote(grad_hbm.at[upper], tokens.at[1, upper], peer(2)))
    from_y.append(remote(grad_hbm.at[lower], tokens.at[2, lower], peer(4)))

    depth = inputs_ref.shape[1]
    low_parts[0] = jnp.dot(
        inputs_ref[...],
        first_ref[pl.ds(pl.multiple_of(z * depth, depth), depth), :],
        preferred_element_type=f32,
    ).astype(bf16)
    low_copies = [remote(low_parts.at[0], low_parts.at[r], over(r)) for r in range(1, 4)]

    own_rows = pl.ds(pl.multiple_of(dp * rows, rows), rows)
    codes_copy.wait()
    pre_copy.wait()
    own_copy.wait()

    def dequantize(step, carry):
        columns = pl.ds(pl.multiple_of(step * tile, tile), tile)
        scales = scales_ref[...]
        high = scales.astype(bf16)
        rest = scales - high.astype(f32)
        middle = rest.astype(bf16)
        last = (rest - middle.astype(f32)).astype(bf16)
        shape = (scales.shape[1], tile)
        place = lax.broadcasted_iota(jnp.int32, shape, 1) // block + step * (tile // block)
        spread = jnp.where(lax.broadcasted_iota(jnp.int32, shape, 0) == place, 1.0, 0.0).astype(bf16)
        expanded = (
            jnp.dot(high, spread, preferred_element_type=f32)
            + jnp.dot(middle, spread, preferred_element_type=f32)
            + jnp.dot(last, spread, preferred_element_type=f32)
        )
        adapter = jnp.dot(first_ref[own_rows, :], second_ref[:, columns], preferred_element_type=f32)
        merged = (
            (codes[:, columns].astype(f32) - 7.5) * expanded + adapter_scale_factor * adapter
        ).astype(bf16)
        weight[core, :, columns] = merged
        merged_f = merged.astype(f32)
        stats[0, 0:1, columns] = jnp.sum(merged_f * merged_f, axis=0, keepdims=True)
        stats[0, 1:2, columns] = jnp.sum(
            tokens[0, :, columns].astype(f32) * pre[:, columns].astype(f32), axis=0, keepdims=True
        )
        return carry

    lax.fori_loop(0, steps, dequantize, 0)

    stats_copies = [remote(stats.at[0], stats.at[o], peer(o)) for o in range(1, 8)]
    weight_index = used[0]
    remote(weight.at[core], weight.at[core], peer(1))
    weight_arrival = arrival(weight.at[core], weight.at[1 - core], weight_index, peer(1))

    for copy in low_copies:
        copy.wait_recv()
    low[0] = (
        (low_parts[0].astype(f32) + low_parts[1].astype(f32))
        + (low_parts[2].astype(f32) + low_parts[3].astype(f32))
    ).astype(bf16)
    plane_low = [remote(low.at[0], low.at[b], peer(2 * b)) for b in range(1, 4)]

    from_x[0].wait_recv()
    far_lower = remote(tokens.at[1, lower], tokens.at[3, lower], peer(4))
    from_y[0].wait_recv()
    far_upper = remote(tokens.at[2, upper], tokens.at[3, upper], peer(2))

    for copy in stats_copies:
        copy.wait_recv()
    total = ((stats[0] + stats[1]) + (stats[2] + stats[3])) + (
        (stats[4] + stats[5]) + (stats[6] + stats[7])
    )
    norm = jnp.sqrt(total[0:1, :] + 1e-06)
    factor[...] = magnitude_ref[...] / norm
    magnitude_out[...] = total[1:2, :] / norm

    weight_arrival.wait_recv()

    across_sends = []
    across_index = used[0]
    used[0] += 8

    def across_copy(which, source, target_slot, to_z):
        return pltpu.make_async_remote_copy(
            src_ref=source,
            dst_ref=across.at[target_slot],
            send_sem=send_sem.at[across_index + which],
            recv_sem=recv_sem.at[across_index + target_slot],
            device_id={"dp": dp, "tensor": to_z},
            device_id_type=MESH,
        )

    def send_across(which):
        quarter_high, quarter_low = flip(y, which // 2), flip(x, which % 2)
        to_z = quarter_high * 2 + quarter_low
        slot = flip(quarter_high, z_high) * 2 + flip(quarter_low, z_low)
        copy = across_copy(which, returned.at[which], slot, to_z)

        @pl.when(to_z != z)
        def _():
            copy.start()

        across_sends.append((copy, to_z))

    nt = (((1,), (1,)), ((), ()))
    tn = (((0,), (0,)), ((), ()))

    def multiply(which, destination):
        acc[...] = jnp.zeros_like(acc)
        if which == 0:
            back_acc[...] = jnp.zeros_like(back_acc)

        def body(step, carry):
            columns = pl.ds(pl.multiple_of(step * tile, tile), tile)
            scaled = (tokens[which, :, columns].astype(f32) * factor[:, columns]).astype(bf16)
            for side in range(2):
                acc[side] += lax.dot_general(
                    scaled, weight[side, :, columns], nt, preferred_element_type=f32
                )
            second_parts[which, :, columns] = lax.dot_general(
                low[which], scaled, tn, preferred_element_type=f32
            )
            if which == 0:
                back_acc[...] += lax.dot_general(
                    scaled, second_ref[:, columns], nt, preferred_element_type=f32
                )
            return carry

        lax.fori_loop(0, steps, body, 0)
        for side in range(2):
            destination[:, pl.ds(side * rows, rows)] = acc[side].astype(bf16)

    multiply(0, returned.at[0])
    send_across(0)
    back_parts[0] = back_acc[...].astype(bf16)
    back_copies = [remote(back_parts.at[0], back_parts.at[r], over(r)) for r in range(1, 4)]

    returns = {}
    from_x[1].wait_recv()
    plane_low[0].wait_recv()
    multiply(1, product.at[0])
    returns[1] = remote(product.at[0], returned.at[1], peer(2))

    for copy in back_copies:
        copy.wait_recv()
    back = (
        (back_parts[0].astype(f32) + back_parts[1].astype(f32))
        + (back_parts[2].astype(f32) + back_parts[3].astype(f32))
    ).astype(bf16)
    slices = first_split.shape[0]
    piece = rank // slices
    gradient = adapter_scale_factor * lax.dot_general(
        back, inputs_ref[...], tn, preferred_element_type=f32
    )
    for index in range(slices):
        first_split[index] = gradient[index * piece : (index + 1) * piece, :]
    first_copies = [
        remote(first_split.at[plane(o)], first_recv.at[o], peer(o)) for o in range(1, 8)
    ]

    from_y[1].wait_recv()
    plane_low[1].wait_recv()
    multiply(2, product.at[1])
    returns[2] = remote(product.at[1], returned.at[2], peer(4))

    for copy in first_copies:
        copy.wait_recv()
    first_recv[0] = first_split[dp]
    first_full[dp] = (
        (first_recv[0] + first_recv[1]) + (first_recv[2] + first_recv[3])
    ) + ((first_recv[4] + first_recv[5]) + (first_recv[6] + first_recv[7]))
    first_index = used[0]
    for o in range(1, 8):
        remote(first_full.at[dp], first_full.at[dp], peer(o))

    returns[1].wait_recv()
    send_across(1)
    returns[2].wait_recv()
    send_across(2)

    far_lower.wait_recv()
    far_upper.wait_recv()
    plane_low[2].wait_recv()
    multiply(3, product.at[2])
    returns[3] = remote(product.at[2], returned.at[3], peer(6))

    second_pair[0] = (second_parts[0] + second_parts[1]) + (second_parts[2] + second_parts[3])
    pair_copy = remote(second_pair.at[0], second_pair.at[1], peer(1))

    for o in range(1, 8):
        arrival(
            first_full.at[dp], first_full.at[plane(o)], first_index + o - 1, peer(o)
        ).wait_recv()
    first_out[...] = jnp.transpose(first_full[...].reshape(rank, depth))

    returns[3].wait_recv()
    send_across(3)

    pair_copy.wait_recv()
    second_out[...] = adapter_scale_factor * (second_pair[0] + second_pair[1])

    for slot in range(1, 4):
        across_copy(slot, returned.at[slot], slot, stack(slot)).wait_recv()
    mine = flip(z_high, y) * 2 + flip(z_low, x)
    out_ref[...] = (
        (returned[mine].astype(f32) + across[1].astype(f32))
        + (across[2].astype(f32) + across[3].astype(f32))
    ).astype(bf16)

    for copy in sent:
        copy.wait_send()
    for copy, to_z in across_sends:

        @pl.when(to_z != z)
        def _(copy=copy):
            copy.wait_send()


def on_device_fused(
    base_codes,
    block_scales,
    input_adapter_factor,
    output_adapter_factor,
    magnitude,
    inputs,
    grad_out,
    pre_scale,
):
    f32, bf16 = jnp.float32, jnp.bfloat16
    rows, width = base_codes.shape
    count, depth = inputs.shape
    rank = input_adapter_factor.shape[1]
    whole = pl.BlockSpec(memory_space=pltpu.VMEM)
    away = pl.BlockSpec(memory_space=pl.ANY)
    grad_inputs, first, second, grad_magnitude = pl.pallas_call(
        fused_kernel,
        out_shape=(
            jax.ShapeDtypeStruct((count, depth), bf16),
            jax.ShapeDtypeStruct((depth, rank), f32),
            jax.ShapeDtypeStruct((rank, width), f32),
            jax.ShapeDtypeStruct((1, width), f32),
        ),
        in_specs=[away, whole, whole, whole, whole, whole, away, away],
        out_specs=(whole, whole, whole, whole),
        scratch_shapes=[
            pltpu.VMEM((rows, width), jnp.int32),
            pltpu.VMEM((count, width), bf16),
            pltpu.VMEM((4, count, width), bf16),
            pltpu.VMEM((2, rows, width), bf16),
            pltpu.VMEM((8, 2, width), f32),
            pltpu.VMEM((1, width), f32),
            pltpu.VMEM((4, count, rank), bf16),
            pltpu.VMEM((4, count, rank), bf16),
            pltpu.VMEM((4, count, rank), bf16),
            pltpu.VMEM((count, rank), f32),
            pltpu.VMEM((2, count, rows), f32),
            pltpu.VMEM((3, count, depth), bf16),
            pltpu.VMEM((4, count, depth), bf16),
            pltpu.VMEM((4, count, depth), bf16),
            pltpu.VMEM((4, rank, width), f32),
            pltpu.VMEM((2, rank, width), f32),
            pltpu.VMEM((8, rank // 8, depth), f32),
            pltpu.VMEM((8, rank // 8, depth), f32),
            pltpu.VMEM((8, rank // 8, depth), f32),
            pltpu.SemaphoreType.DMA((3,)),
            pltpu.SemaphoreType.DMA((64,)),
            pltpu.SemaphoreType.DMA((64,)),
        ],
        compiler_params=pltpu.CompilerParams(
            collective_id=0, has_side_effects=True, vmem_limit_bytes=58 * 1024 * 1024
        ),
    )(
        base_codes,
        block_scales,
        input_adapter_factor,
        output_adapter_factor,
        magnitude.reshape(1, width),
        inputs,
        grad_out,
        pre_scale,
    )
    return grad_inputs, first, second, grad_magnitude.reshape(width)


def solution(mesh):
    fits = mesh.shape["dp"] == 8 and mesh.shape["tensor"] == 4
    body = on_device_fused if fits else on_device
    in_specs = (
        P("dp", "tensor"),
        P("dp", "tensor"),
        P(),
        P(None, "tensor"),
        P("tensor"),
        P("dp", "tensor"),
        P("dp", "tensor"),
        P("dp", "tensor"),
    )
    out_specs = (P("dp", "tensor"), P("tensor", None), P(None, "tensor"), P("tensor"))
    return jax.shard_map(
        body, mesh=mesh, in_specs=in_specs, out_specs=out_specs, check_vma=False
    )
```

```python
import jax
import jax.numpy as jnp
from jax import lax
from jax.experimental import pallas as pl
from jax.experimental.pallas import tpu as pltpu
from jax.sharding import PartitionSpec as P

adapter_scale_factor = 0.5


def on_device(
    base_codes,
    block_scales,
    input_adapter_factor,
    output_adapter_factor,
    magnitude,
    inputs,
    grad_out,
    pre_scale,
):
    f32, bf16 = jnp.float32, jnp.bfloat16
    row_count, columns = base_codes.shape
    tokens = grad_out.shape[0]
    dp = lax.axis_index("dp")
    block_size = columns // block_scales.shape[1]
    gathered = lax.all_gather(grad_out, "dp", axis=0, tiled=True)
    quarter_d = inputs.shape[1]
    adapter_part = lax.dynamic_slice_in_dim(
        input_adapter_factor, lax.axis_index("tensor") * quarter_d, quarter_d, 0
    )
    hidden_low = lax.psum(
        jnp.dot(inputs, adapter_part, preferred_element_type=f32).astype(bf16), "tensor"
    )
    hidden_all = lax.all_gather(hidden_low, "dp", axis=0, tiled=True)
    expanded = jnp.repeat(block_scales, block_size, axis=1)
    adapter_row_block = lax.dynamic_slice_in_dim(
        input_adapter_factor, dp * row_count, row_count, 0
    )
    merged = (
        (base_codes.astype(f32) - 7.5) * expanded
        + adapter_scale_factor
        * jnp.dot(adapter_row_block, output_adapter_factor, preferred_element_type=f32)
    ).astype(bf16)
    merged_f = merged.astype(f32)
    column_sums = jnp.sum(merged_f * merged_f, axis=0)
    magnitude_sums = jnp.sum(grad_out.astype(f32) * pre_scale.astype(f32), axis=0)
    column_sums, magnitude_sums = lax.psum((column_sums, magnitude_sums), "dp")
    col_norm = jnp.sqrt(column_sums + 1e-06)
    scaled = (gathered.astype(f32) * (magnitude / col_norm)).astype(bf16)
    partial_value = jnp.einsum("tf,rf->tr", scaled, merged, preferred_element_type=f32)
    exchanged = lax.all_to_all(
        partial_value.astype(bf16), "dp", split_axis=0, concat_axis=1, tiled=True
    )
    grad_inputs = lax.psum_scatter(exchanged, "tensor", scatter_dimension=1, tiled=True)
    own_scaled = lax.dynamic_slice_in_dim(scaled, dp * tokens, tokens, 0)
    back_low = lax.psum(
        jnp.einsum(
            "tf,rf->tr", own_scaled, output_adapter_factor, preferred_element_type=f32
        ).astype(bf16),
        "tensor",
    )
    input_gradient = lax.psum(
        adapter_scale_factor
        * jnp.einsum("td,tr->dr", inputs, back_low, preferred_element_type=f32),
        "dp",
    )
    output_gradient = adapter_scale_factor * jnp.einsum(
        "tr,tf->rf", hidden_all, scaled, preferred_element_type=f32
    )
    return (grad_inputs, input_gradient, output_gradient, magnitude_sums / col_norm)


MESH = pl.DeviceIdType.MESH
COLUMN_TILE = 512


def flip(bit, by):
    return bit + by - 2 * bit * by


def fused_kernel(
    codes_hbm,
    scales_ref,
    first_ref,
    second_ref,
    magnitude_ref,
    inputs_ref,
    grad_hbm,
    pre_hbm,
    out_ref,
    first_out,
    second_out,
    magnitude_out,
    codes,
    pre,
    tokens,
    weight,
    stats,
    factor,
    low_parts,
    low,
    back_parts,
    back_acc,
    acc,
    product,
    returned,
    arriving,
    second_parts,
    second_pair,
    pieces,
    adapter_rows,
    first_split,
    first_recv,
    first_full,
    local_sem,
    send_sem,
    recv_sem,
):
    f32, bf16 = jnp.float32, jnp.bfloat16
    rows, width = codes.shape
    count = tokens.shape[1]
    half = count // 2
    tile = COLUMN_TILE
    steps = width // tile
    rank = low.shape[2]
    block = width // scales_ref.shape[0]
    dp, z = lax.axis_index("dp"), lax.axis_index("tensor")
    core = lax.rem(dp, 2)
    x = lax.rem(dp // 2, 2)
    y = dp // 4
    z_low, z_high = lax.rem(z, 2), z // 2

    def plane(offset):
        return (
            flip(y, offset // 4) * 4 + flip(x, (offset // 2) % 2) * 2 + flip(core, offset % 2)
        )

    def stack(offset):
        return flip(z_high, offset // 2) * 2 + flip(z_low, offset % 2)

    used = [0]
    sent = []

    def remote(source, target, to, start=True):
        index = used[0]
        used[0] += 1
        copy = pltpu.make_async_remote_copy(
            src_ref=source,
            dst_ref=target,
            send_sem=send_sem.at[index],
            recv_sem=recv_sem.at[index],
            device_id=to,
            device_id_type=MESH,
        )
        copy.start()
        sent.append(copy)
        return copy

    def arrival(source, target, copy_index, to):
        return pltpu.make_async_remote_copy(
            src_ref=source,
            dst_ref=target,
            send_sem=send_sem.at[copy_index],
            recv_sem=recv_sem.at[copy_index],
            device_id=to,
            device_id_type=MESH,
        )

    def peer(offset):
        return {"dp": plane(offset), "tensor": z}

    def over(offset):
        return {"dp": dp, "tensor": stack(offset)}

    codes_copy = pltpu.make_async_copy(codes_hbm, codes, local_sem.at[0])
    pre_copy = pltpu.make_async_copy(pre_hbm, pre, local_sem.at[1])
    own_copy = pltpu.make_async_copy(grad_hbm, tokens.at[0], local_sem.at[2])
    codes_copy.start()
    pre_copy.start()
    own_copy.start()

    barrier = pltpu.get_barrier_semaphore()
    for offset in range(1, 8):
        pl.semaphore_signal(barrier, inc=1, device_id=peer(offset), device_id_type=MESH)
    for offset in range(1, 4):
        pl.semaphore_signal(barrier, inc=1, device_id=over(offset), device_id_type=MESH)
    pl.semaphore_wait(barrier, 10)

    lower, upper = pl.ds(0, half), pl.ds(half, half)
    from_x = [
        remote(grad_hbm.at[lower], tokens.at[1, lower], peer(2)),
    ]
    from_y = [
        remote(grad_hbm.at[upper], tokens.at[2, upper], peer(4)),
    ]
    from_x.append(remote(grad_hbm.at[upper], tokens.at[1, upper], peer(2)))
    from_y.append(remote(grad_hbm.at[lower], tokens.at[2, lower], peer(4)))

    depth = inputs_ref.shape[1]
    nt = (((1,), (1,)), ((), ()))
    tn = (((0,), (0,)), ((), ()))
    low_parts[0] = lax.dot_general(
        inputs_ref[...],
        first_ref[:, pl.ds(pl.multiple_of(z * depth, depth), depth)],
        nt,
        preferred_element_type=f32,
    ).astype(bf16)
    low_copies = [remote(low_parts.at[0], low_parts.at[r], over(r)) for r in range(1, 4)]

    own_rows = pl.ds(pl.multiple_of(dp * rows, rows), rows)
    adapter_rows[...] = jnp.transpose(first_ref[:, own_rows].astype(f32)).astype(bf16)
    scales = jnp.transpose(scales_ref[...])
    high = scales.astype(bf16)
    rest = scales - high.astype(f32)
    middle = rest.astype(bf16)
    pieces[0] = high
    pieces[1] = middle
    pieces[2] = (rest - middle.astype(f32)).astype(bf16)
    codes_copy.wait()
    pre_copy.wait()
    own_copy.wait()

    def dequantize(step, carry):
        columns = pl.ds(pl.multiple_of(step * tile, tile), tile)
        shape = (scales_ref.shape[0], tile)
        place = lax.broadcasted_iota(jnp.int32, shape, 1) // block + step * (tile // block)
        spread = jnp.where(lax.broadcasted_iota(jnp.int32, shape, 0) == place, 1.0, 0.0).astype(bf16)
        expanded = (
            jnp.dot(pieces[0], spread, preferred_element_type=f32)
            + jnp.dot(pieces[1], spread, preferred_element_type=f32)
            + jnp.dot(pieces[2], spread, preferred_element_type=f32)
        )
        adapter = jnp.dot(adapter_rows[...], second_ref[:, columns], preferred_element_type=f32)
        merged = (
            (codes[:, columns].astype(f32) - 7.5) * expanded + adapter_scale_factor * adapter
        ).astype(bf16)
        weight[core, :, columns] = merged
        merged_f = merged.astype(f32)
        stats[0, 0:1, columns] = jnp.sum(merged_f * merged_f, axis=0, keepdims=True)
        stats[0, 1:2, columns] = jnp.sum(
            tokens[0, :, columns].astype(f32) * pre[:, columns].astype(f32), axis=0, keepdims=True
        )
        return carry

    lax.fori_loop(0, steps, dequantize, 0)

    stats_copies = [remote(stats.at[0], stats.at[o], peer(o)) for o in range(1, 8)]
    weight_index = used[0]
    remote(weight.at[core], weight.at[core], peer(1))
    weight_arrival = arrival(weight.at[core], weight.at[1 - core], weight_index, peer(1))

    for copy in low_copies:
        copy.wait_recv()
    low[0] = (
        (low_parts[0].astype(f32) + low_parts[1].astype(f32))
        + (low_parts[2].astype(f32) + low_parts[3].astype(f32))
    ).astype(bf16)
    plane_low = [remote(low.at[0], low.at[b], peer(2 * b)) for b in range(1, 4)]

    from_x[0].wait_recv()
    far_lower = remote(tokens.at[1, lower], tokens.at[3, lower], peer(4))
    from_y[0].wait_recv()
    far_upper = remote(tokens.at[2, upper], tokens.at[3, upper], peer(2))

    for copy in stats_copies:
        copy.wait_recv()
    total = ((stats[0] + stats[1]) + (stats[2] + stats[3])) + (
        (stats[4] + stats[5]) + (stats[6] + stats[7])
    )
    norm = jnp.sqrt(total[0:1, :] + 1e-06)
    factor[...] = magnitude_ref[...].reshape(1, width) / norm
    magnitude_out[...] = (total[1:2, :] / norm).reshape(width)

    weight_arrival.wait_recv()

    halves = (lower, upper)
    chain_sends = []
    chain_index = used[0]
    used[0] += 16

    def chain_copy(which, part, side, to_z):
        return pltpu.make_async_remote_copy(
            src_ref=returned.at[which, halves[part]],
            dst_ref=arriving.at[side, which, halves[part]],
            send_sem=send_sem.at[chain_index + which * 2 + part],
            recv_sem=recv_sem.at[chain_index + (side * 4 + which) * 2 + part],
            device_id={"dp": dp, "tensor": to_z},
            device_id_type=MESH,
        )

    def chain(which, part):
        owner = flip(y, which // 2) * 2 + flip(x, which % 2)
        for side in range(2):
            toward, last = ((1, 0), (-1, 3))[side]
            copy = chain_copy(which, part, side, lax.rem(z + toward + 4, 4))
            active = z < owner if side == 0 else z > owner

            @pl.when(active)
            def _(copy=copy, side=side, last=last):
                @pl.when(z != last)
                def _():
                    copy.wait_recv()
                    returned[which, halves[part]] = (
                        returned[which, halves[part]].astype(f32)
                        + arriving[side, which, halves[part]].astype(f32)
                    ).astype(bf16)

                copy.start()

            chain_sends.append((copy, active))

    def multiply(which, destination, start, size, second):
        part = pl.ds(start, size)
        acc[:, part] = jnp.zeros((2, size, rows), f32)
        if which == 0:
            back_acc[...] = jnp.zeros_like(back_acc)

        def body(step, carry):
            columns = pl.ds(pl.multiple_of(step * tile, tile), tile)
            if second:
                scaled = (tokens[which, :, columns].astype(f32) * factor[:, columns]).astype(bf16)
                second_parts[which, :, columns] = lax.dot_general(
                    low[which], scaled, tn, preferred_element_type=f32
                )
                piece = scaled[start : start + size, :]
            else:
                piece = (tokens[which, part, columns].astype(f32) * factor[:, columns]).astype(bf16)
            for side in range(2):
                acc[side, part] += lax.dot_general(
                    piece, weight[side, :, columns], nt, preferred_element_type=f32
                )
            if which == 0:
                back_acc[...] += lax.dot_general(
                    scaled, second_ref[:, columns], nt, preferred_element_type=f32
                )
            return carry

        lax.fori_loop(0, steps, body, 0)
        for side in range(2):
            destination[part, pl.ds(side * rows, rows)] = acc[side, part].astype(bf16)

    multiply(0, returned.at[0], 0, count, True)
    back_parts[0] = back_acc[...].astype(bf16)
    back_copies = [remote(back_parts.at[0], back_parts.at[r], over(r)) for r in range(1, 4)]

    returns = {}
    from_x[1].wait_recv()
    plane_low[0].wait_recv()
    multiply(1, product.at[0], 0, count, True)
    returns[1] = remote(product.at[0], returned.at[1], peer(2))
    chain(0, 0)
    chain(0, 1)

    for copy in back_copies:
        copy.wait_recv()
    back = (
        (back_parts[0].astype(f32) + back_parts[1].astype(f32))
        + (back_parts[2].astype(f32) + back_parts[3].astype(f32))
    ).astype(bf16)
    slices = first_split.shape[0]
    piece = rank // slices
    gradient = adapter_scale_factor * lax.dot_general(
        back, inputs_ref[...], tn, preferred_element_type=f32
    )
    for index in range(slices):
        first_split[index] = gradient[index * piece : (index + 1) * piece, :]
    first_copies = [
        remote(first_split.at[plane(o)], first_recv.at[o], peer(o)) for o in range(1, 8)
    ]

    from_y[1].wait_recv()
    plane_low[1].wait_recv()
    multiply(2, product.at[1], 0, count, True)
    returns[2] = remote(product.at[1], returned.at[2], peer(4))

    for copy in first_copies:
        copy.wait_recv()
    first_recv[0] = first_split[dp]
    first_full[dp] = (
        (first_recv[0] + first_recv[1]) + (first_recv[2] + first_recv[3])
    ) + ((first_recv[4] + first_recv[5]) + (first_recv[6] + first_recv[7]))
    first_index = used[0]
    for o in range(1, 8):
        remote(first_full.at[dp], first_full.at[dp], peer(o))

    far_lower.wait_recv()
    multiply(3, product.at[2], 0, half, False)
    far_returns = [remote(product.at[2, lower], returned.at[3, lower], peer(6))]
    far_upper.wait_recv()
    plane_low[2].wait_recv()
    multiply(3, product.at[2], half, half, True)
    far_returns.append(remote(product.at[2, upper], returned.at[3, upper], peer(6)))

    returns[1].wait_recv()
    chain(1, 0)
    chain(1, 1)
    returns[2].wait_recv()
    chain(2, 0)
    chain(2, 1)

    far_returns[0].wait_recv()
    chain(3, 0)
    far_returns[1].wait_recv()
    chain(3, 1)

    second_pair[0] = (second_parts[0] + second_parts[1]) + (second_parts[2] + second_parts[3])
    pair_copy = remote(second_pair.at[0], second_pair.at[1], peer(1))

    for o in range(1, 8):
        arrival(
            first_full.at[dp], first_full.at[plane(o)], first_index + o - 1, peer(o)
        ).wait_recv()
    first_out[...] = first_full[...].reshape(rank, depth)

    pair_copy.wait_recv()
    second_out[...] = adapter_scale_factor * (second_pair[0] + second_pair[1])

    mine = flip(z_high, y) * 2 + flip(z_low, x)
    for part in range(2):
        rows_here = halves[part]
        acc[:, rows_here] = jnp.zeros((2, half, rows), f32)
        for side in range(2):
            copy = chain_copy(mine, part, side, lax.rem(z + 1, 4))

            @pl.when(z != (0, 3)[side])
            def _(copy=copy, side=side, rows_here=rows_here):
                copy.wait_recv()
                for column in range(2):
                    place = pl.ds(column * rows, rows)
                    acc[column, rows_here] += arriving[side, mine, rows_here, place].astype(f32)

        for column in range(2):
            place = pl.ds(column * rows, rows)
            out_ref[rows_here, place] = (
                acc[column, rows_here] + returned[mine, rows_here, place].astype(f32)
            ).astype(bf16)

    for copy in sent:
        copy.wait_send()
    for copy, active in chain_sends:

        @pl.when(active)
        def _(copy=copy):
            copy.wait_send()


def on_device_fused(
    base_codes,
    block_scales,
    input_adapter_factor,
    output_adapter_factor,
    magnitude,
    inputs,
    grad_out,
    pre_scale,
):
    f32, bf16 = jnp.float32, jnp.bfloat16
    rows, width = base_codes.shape
    count, depth = inputs.shape
    rank = input_adapter_factor.shape[1]
    whole = pl.BlockSpec(memory_space=pltpu.VMEM)
    away = pl.BlockSpec(memory_space=pl.ANY)
    grad_inputs, first, second, grad_magnitude = pl.pallas_call(
        fused_kernel,
        out_shape=(
            jax.ShapeDtypeStruct((count, depth), bf16),
            jax.ShapeDtypeStruct((rank, depth), f32),
            jax.ShapeDtypeStruct((rank, width), f32),
            jax.ShapeDtypeStruct((width,), f32),
        ),
        in_specs=[away, whole, whole, whole, whole, whole, away, away],
        out_specs=(whole, whole, whole, whole),
        scratch_shapes=[
            pltpu.VMEM((rows, width), jnp.int32),
            pltpu.VMEM((count, width), bf16),
            pltpu.VMEM((4, count, width), bf16),
            pltpu.VMEM((2, rows, width), bf16),
            pltpu.VMEM((8, 2, width), f32),
            pltpu.VMEM((1, width), f32),
            pltpu.VMEM((4, count, rank), bf16),
            pltpu.VMEM((4, count, rank), bf16),
            pltpu.VMEM((4, count, rank), bf16),
            pltpu.VMEM((count, rank), f32),
            pltpu.VMEM((2, count, rows), f32),
            pltpu.VMEM((3, count, depth), bf16),
            pltpu.VMEM((4, count, depth), bf16),
            pltpu.VMEM((2, 4, count, depth), bf16),
            pltpu.VMEM((4, rank, width), f32),
            pltpu.VMEM((2, rank, width), f32),
            pltpu.VMEM((3, rows, block_scales.shape[1]), bf16),
            pltpu.VMEM((rows, rank), bf16),
            pltpu.VMEM((8, rank // 8, depth), f32),
            pltpu.VMEM((8, rank // 8, depth), f32),
            pltpu.VMEM((8, rank // 8, depth), f32),
            pltpu.SemaphoreType.DMA((3,)),
            pltpu.SemaphoreType.DMA((72,)),
            pltpu.SemaphoreType.DMA((72,)),
        ],
        compiler_params=pltpu.CompilerParams(
            collective_id=0, has_side_effects=True, vmem_limit_bytes=58 * 1024 * 1024
        ),
    )(
        base_codes,
        block_scales.T,
        input_adapter_factor.T,
        output_adapter_factor,
        magnitude,
        inputs,
        grad_out,
        pre_scale,
    )
    return grad_inputs, first.T, second, grad_magnitude


def solution(mesh):
    fits = mesh.shape["dp"] == 8 and mesh.shape["tensor"] == 4
    body = on_device_fused if fits else on_device
    in_specs = (
        P("dp", "tensor"),
        P("dp", "tensor"),
        P(),
        P(None, "tensor"),
        P("tensor"),
        P("dp", "tensor"),
        P("dp", "tensor"),
        P("dp", "tensor"),
    )
    out_specs = (P("dp", "tensor"), P("tensor", None), P(None, "tensor"), P("tensor"))
    return jax.shard_map(
        body, mesh=mesh, in_specs=in_specs, out_specs=out_specs, check_vma=False
    )
```

```python
import jax
import jax.numpy as jnp
from jax import lax
from jax.experimental import pallas as pl
from jax.experimental.pallas import tpu as pltpu
from jax.sharding import PartitionSpec as P

adapter_scale_factor = 0.5


def on_device(
    base_codes,
    block_scales,
    input_adapter_factor,
    output_adapter_factor,
    magnitude,
    inputs,
    grad_out,
    pre_scale,
):
    f32, bf16 = jnp.float32, jnp.bfloat16
    row_count, columns = base_codes.shape
    tokens = grad_out.shape[0]
    dp = lax.axis_index("dp")
    block_size = columns // block_scales.shape[1]
    gathered = lax.all_gather(grad_out, "dp", axis=0, tiled=True)
    quarter_d = inputs.shape[1]
    adapter_part = lax.dynamic_slice_in_dim(
        input_adapter_factor, lax.axis_index("tensor") * quarter_d, quarter_d, 0
    )
    hidden_low = lax.psum(
        jnp.dot(inputs, adapter_part, preferred_element_type=f32).astype(bf16), "tensor"
    )
    hidden_all = lax.all_gather(hidden_low, "dp", axis=0, tiled=True)
    expanded = jnp.repeat(block_scales, block_size, axis=1)
    adapter_row_block = lax.dynamic_slice_in_dim(
        input_adapter_factor, dp * row_count, row_count, 0
    )
    merged = (
        (base_codes.astype(f32) - 7.5) * expanded
        + adapter_scale_factor
        * jnp.dot(adapter_row_block, output_adapter_factor, preferred_element_type=f32)
    ).astype(bf16)
    merged_f = merged.astype(f32)
    column_sums = jnp.sum(merged_f * merged_f, axis=0)
    magnitude_sums = jnp.sum(grad_out.astype(f32) * pre_scale.astype(f32), axis=0)
    column_sums, magnitude_sums = lax.psum((column_sums, magnitude_sums), "dp")
    col_norm = jnp.sqrt(column_sums + 1e-06)
    scaled = (gathered.astype(f32) * (magnitude / col_norm)).astype(bf16)
    partial_value = jnp.einsum("tf,rf->tr", scaled, merged, preferred_element_type=f32)
    exchanged = lax.all_to_all(
        partial_value.astype(bf16), "dp", split_axis=0, concat_axis=1, tiled=True
    )
    grad_inputs = lax.psum_scatter(exchanged, "tensor", scatter_dimension=1, tiled=True)
    own_scaled = lax.dynamic_slice_in_dim(scaled, dp * tokens, tokens, 0)
    back_low = lax.psum(
        jnp.einsum(
            "tf,rf->tr", own_scaled, output_adapter_factor, preferred_element_type=f32
        ).astype(bf16),
        "tensor",
    )
    input_gradient = lax.psum(
        adapter_scale_factor
        * jnp.einsum("td,tr->dr", inputs, back_low, preferred_element_type=f32),
        "dp",
    )
    output_gradient = adapter_scale_factor * jnp.einsum(
        "tr,tf->rf", hidden_all, scaled, preferred_element_type=f32
    )
    return (grad_inputs, input_gradient, output_gradient, magnitude_sums / col_norm)


MESH = pl.DeviceIdType.MESH
COLUMN_TILE = 512


def flip(bit, by):
    return bit + by - 2 * bit * by


def fused_kernel(
    codes_hbm,
    scales_ref,
    first_ref,
    second_ref,
    magnitude_ref,
    inputs_ref,
    grad_hbm,
    pre_hbm,
    out_ref,
    first_out,
    second_out,
    magnitude_out,
    codes,
    pre,
    tokens,
    weight,
    stats,
    factor,
    low_parts,
    low,
    back_parts,
    back_acc,
    acc,
    product,
    shares,
    summed,
    returned,
    final,
    second_parts,
    second_pair,
    pieces,
    adapter_rows,
    first_split,
    first_recv,
    first_full,
    local_sem,
    send_sem,
    recv_sem,
):
    f32, bf16 = jnp.float32, jnp.bfloat16
    rows, width = codes.shape
    count = tokens.shape[1]
    half = count // 2
    tile = COLUMN_TILE
    steps = width // tile
    rank = low.shape[2]
    block = width // scales_ref.shape[0]
    dp, z = lax.axis_index("dp"), lax.axis_index("tensor")
    core = lax.rem(dp, 2)
    x = lax.rem(dp // 2, 2)
    y = dp // 4
    z_low, z_high = lax.rem(z, 2), z // 2

    def plane(offset):
        return (
            flip(y, offset // 4) * 4 + flip(x, (offset // 2) % 2) * 2 + flip(core, offset % 2)
        )

    def stack(offset):
        return flip(z_high, offset // 2) * 2 + flip(z_low, offset % 2)

    used = [0]
    sent = []

    def remote(source, target, to, start=True):
        index = used[0]
        used[0] += 1
        copy = pltpu.make_async_remote_copy(
            src_ref=source,
            dst_ref=target,
            send_sem=send_sem.at[index],
            recv_sem=recv_sem.at[index],
            device_id=to,
            device_id_type=MESH,
        )
        copy.start()
        sent.append(copy)
        return copy

    def arrival(source, target, copy_index, to):
        return pltpu.make_async_remote_copy(
            src_ref=source,
            dst_ref=target,
            send_sem=send_sem.at[copy_index],
            recv_sem=recv_sem.at[copy_index],
            device_id=to,
            device_id_type=MESH,
        )

    def peer(offset):
        return {"dp": plane(offset), "tensor": z}

    def over(offset):
        return {"dp": dp, "tensor": stack(offset)}

    codes_copy = pltpu.make_async_copy(codes_hbm, codes, local_sem.at[0])
    pre_copy = pltpu.make_async_copy(pre_hbm, pre, local_sem.at[1])
    own_copy = pltpu.make_async_copy(grad_hbm, tokens.at[0], local_sem.at[2])
    codes_copy.start()
    pre_copy.start()
    own_copy.start()

    barrier = pltpu.get_barrier_semaphore()
    for offset in range(1, 8):
        pl.semaphore_signal(barrier, inc=1, device_id=peer(offset), device_id_type=MESH)
    for offset in range(1, 4):
        pl.semaphore_signal(barrier, inc=1, device_id=over(offset), device_id_type=MESH)
    pl.semaphore_wait(barrier, 10)

    lower, upper = pl.ds(0, half), pl.ds(half, half)
    from_x = [
        remote(grad_hbm.at[lower], tokens.at[1, lower], peer(2)),
    ]
    from_y = [
        remote(grad_hbm.at[upper], tokens.at[2, upper], peer(4)),
    ]
    from_x.append(remote(grad_hbm.at[upper], tokens.at[1, upper], peer(2)))
    from_y.append(remote(grad_hbm.at[lower], tokens.at[2, lower], peer(4)))

    depth = inputs_ref.shape[1]
    nt = (((1,), (1,)), ((), ()))
    tn = (((0,), (0,)), ((), ()))
    low_parts[0] = lax.dot_general(
        inputs_ref[...],
        first_ref[:, pl.ds(pl.multiple_of(z * depth, depth), depth)],
        nt,
        preferred_element_type=f32,
    ).astype(bf16)
    low_copies = [remote(low_parts.at[0], low_parts.at[r], over(r)) for r in range(1, 4)]

    own_rows = pl.ds(pl.multiple_of(dp * rows, rows), rows)
    adapter_rows[...] = jnp.transpose(first_ref[:, own_rows].astype(f32)).astype(bf16)
    scales = jnp.transpose(scales_ref[...])
    high = scales.astype(bf16)
    rest = scales - high.astype(f32)
    middle = rest.astype(bf16)
    pieces[0] = high
    pieces[1] = middle
    pieces[2] = (rest - middle.astype(f32)).astype(bf16)
    codes_copy.wait()
    pre_copy.wait()
    own_copy.wait()

    def dequantize(step, carry):
        columns = pl.ds(pl.multiple_of(step * tile, tile), tile)
        shape = (scales_ref.shape[0], tile)
        place = lax.broadcasted_iota(jnp.int32, shape, 1) // block + step * (tile // block)
        spread = jnp.where(lax.broadcasted_iota(jnp.int32, shape, 0) == place, 1.0, 0.0).astype(bf16)
        expanded = (
            jnp.dot(pieces[0], spread, preferred_element_type=f32)
            + jnp.dot(pieces[1], spread, preferred_element_type=f32)
            + jnp.dot(pieces[2], spread, preferred_element_type=f32)
        )
        adapter = jnp.dot(adapter_rows[...], second_ref[:, columns], preferred_element_type=f32)
        merged = (
            (codes[:, columns].astype(f32) - 7.5) * expanded + adapter_scale_factor * adapter
        ).astype(bf16)
        weight[core, :, columns] = merged
        merged_f = merged.astype(f32)
        stats[0, 0:1, columns] = jnp.sum(merged_f * merged_f, axis=0, keepdims=True)
        stats[0, 1:2, columns] = jnp.sum(
            tokens[0, :, columns].astype(f32) * pre[:, columns].astype(f32), axis=0, keepdims=True
        )
        return carry

    lax.fori_loop(0, steps, dequantize, 0)

    stats_copies = [remote(stats.at[0], stats.at[o], peer(o)) for o in range(1, 8)]
    weight_index = used[0]
    remote(weight.at[core], weight.at[core], peer(1))
    weight_arrival = arrival(weight.at[core], weight.at[1 - core], weight_index, peer(1))

    for copy in low_copies:
        copy.wait_recv()
    low[0] = (
        (low_parts[0].astype(f32) + low_parts[1].astype(f32))
        + (low_parts[2].astype(f32) + low_parts[3].astype(f32))
    ).astype(bf16)
    plane_low = [remote(low.at[0], low.at[b], peer(2 * b)) for b in range(1, 4)]

    from_x[0].wait_recv()
    far_lower = remote(tokens.at[1, lower], tokens.at[3, lower], peer(4))
    from_y[0].wait_recv()
    far_upper = remote(tokens.at[2, upper], tokens.at[3, upper], peer(2))

    for copy in stats_copies:
        copy.wait_recv()
    total = ((stats[0] + stats[1]) + (stats[2] + stats[3])) + (
        (stats[4] + stats[5]) + (stats[6] + stats[7])
    )
    norm = jnp.sqrt(total[0:1, :] + 1e-06)
    factor[...] = magnitude_ref[...].reshape(1, width) / norm
    magnitude_out[...] = (total[1:2, :] / norm).reshape(width)

    weight_arrival.wait_recv()

    part = count // 4

    def part_rows(to_z):
        return pl.ds(pl.multiple_of(to_z * part, part), part)

    def send_shares(which):
        return [
            remote(product.at[which, part_rows(stack(r))], shares.at[which, r], over(r))
            for r in range(1, 4)
        ]

    def sum_shares(which, copies):
        for copy in copies:
            copy.wait_recv()
        target = returned if which == 0 else summed
        target[which] = (
            (product[which, part_rows(z)].astype(f32) + shares[which, 1].astype(f32))
            + (shares[which, 2].astype(f32) + shares[which, 3].astype(f32))
        ).astype(bf16)
        if which == 0:
            return None
        return remote(summed.at[which], returned.at[which], peer(2 * which))

    final_sends = []
    final_index = used[0]
    used[0] += 4

    def final_copy(which, slot, to_z):
        return pltpu.make_async_remote_copy(
            src_ref=returned.at[which],
            dst_ref=final.at[part_rows(z)],
            send_sem=send_sem.at[final_index + which],
            recv_sem=recv_sem.at[final_index + slot],
            device_id={"dp": dp, "tensor": to_z},
            device_id_type=MESH,
        )

    def send_final(which):
        quarter_high, quarter_low = flip(y, which // 2), flip(x, which % 2)
        to_z = quarter_high * 2 + quarter_low
        slot = flip(quarter_high, z_high) * 2 + flip(quarter_low, z_low)
        copy = final_copy(which, slot, to_z)

        @pl.when(to_z != z)
        def _():
            copy.start()

        @pl.when(to_z == z)
        def _():
            final[part_rows(z)] = returned[which]

        final_sends.append((copy, to_z))

    def multiply(which):
        acc[...] = jnp.zeros_like(acc)
        if which == 0:
            back_acc[...] = jnp.zeros_like(back_acc)

        def body(step, carry):
            columns = pl.ds(pl.multiple_of(step * tile, tile), tile)
            scaled = (tokens[which, :, columns].astype(f32) * factor[:, columns]).astype(bf16)
            for side in range(2):
                acc[side] += lax.dot_general(
                    scaled, weight[side, :, columns], nt, preferred_element_type=f32
                )
            second_parts[which, :, columns] = lax.dot_general(
                low[which], scaled, tn, preferred_element_type=f32
            )
            if which == 0:
                back_acc[...] += lax.dot_general(
                    scaled, second_ref[:, columns], nt, preferred_element_type=f32
                )
            return carry

        lax.fori_loop(0, steps, body, 0)
        for side in range(2):
            product[which, :, pl.ds(side * rows, rows)] = acc[side].astype(bf16)
        return send_shares(which)

    shares_0 = multiply(0)
    back_parts[0] = back_acc[...].astype(bf16)
    back_copies = [remote(back_parts.at[0], back_parts.at[r], over(r)) for r in range(1, 4)]

    from_x[1].wait_recv()
    plane_low[0].wait_recv()
    shares_1 = multiply(1)
    sum_shares(0, shares_0)
    send_final(0)

    from_y[1].wait_recv()
    plane_low[1].wait_recv()
    shares_2 = multiply(2)
    return_1 = sum_shares(1, shares_1)

    for copy in back_copies:
        copy.wait_recv()
    back = (
        (back_parts[0].astype(f32) + back_parts[1].astype(f32))
        + (back_parts[2].astype(f32) + back_parts[3].astype(f32))
    ).astype(bf16)
    slices = first_split.shape[0]
    piece = rank // slices
    gradient = adapter_scale_factor * lax.dot_general(
        back, inputs_ref[...], tn, preferred_element_type=f32
    )
    for index in range(slices):
        first_split[index] = gradient[index * piece : (index + 1) * piece, :]

    return_2 = sum_shares(2, shares_2)
    return_1.wait_recv()
    send_final(1)

    far_lower.wait_recv()
    far_upper.wait_recv()
    plane_low[2].wait_recv()
    shares_3 = multiply(3)
    first_copies = [
        remote(first_split.at[plane(o)], first_recv.at[o], peer(o)) for o in range(1, 8)
    ]
    second_pair[0] = (second_parts[0] + second_parts[1]) + (second_parts[2] + second_parts[3])
    pair_copy = remote(second_pair.at[0], second_pair.at[1], peer(1))
    return_2.wait_recv()
    send_final(2)
    return_3 = sum_shares(3, shares_3)

    for copy in first_copies:
        copy.wait_recv()
    first_recv[0] = first_split[dp]
    first_full[dp] = (
        (first_recv[0] + first_recv[1]) + (first_recv[2] + first_recv[3])
    ) + ((first_recv[4] + first_recv[5]) + (first_recv[6] + first_recv[7]))
    first_index = used[0]
    for o in range(1, 8):
        remote(first_full.at[dp], first_full.at[dp], peer(o))

    return_3.wait_recv()
    send_final(3)

    pair_copy.wait_recv()
    second_out[...] = adapter_scale_factor * (second_pair[0] + second_pair[1])
    for o in range(1, 8):
        arrival(
            first_full.at[dp], first_full.at[plane(o)], first_index + o - 1, peer(o)
        ).wait_recv()
    first_out[...] = first_full[...].reshape(rank, depth)

    for slot in range(1, 4):
        pltpu.make_async_remote_copy(
            src_ref=returned.at[slot],
            dst_ref=final.at[part_rows(stack(slot))],
            send_sem=send_sem.at[final_index + slot],
            recv_sem=recv_sem.at[final_index + slot],
            device_id=over(slot),
            device_id_type=MESH,
        ).wait_recv()
    out_ref[...] = final[...]

    for copy in sent:
        copy.wait_send()
    for copy, to_z in final_sends:

        @pl.when(to_z != z)
        def _(copy=copy):
            copy.wait_send()


def on_device_fused(
    base_codes,
    block_scales,
    input_adapter_factor,
    output_adapter_factor,
    magnitude,
    inputs,
    grad_out,
    pre_scale,
):
    f32, bf16 = jnp.float32, jnp.bfloat16
    rows, width = base_codes.shape
    count, depth = inputs.shape
    rank = input_adapter_factor.shape[1]
    whole = pl.BlockSpec(memory_space=pltpu.VMEM)
    away = pl.BlockSpec(memory_space=pl.ANY)
    grad_inputs, first, second, grad_magnitude = pl.pallas_call(
        fused_kernel,
        out_shape=(
            jax.ShapeDtypeStruct((count, depth), bf16),
            jax.ShapeDtypeStruct((rank, depth), f32),
            jax.ShapeDtypeStruct((rank, width), f32),
            jax.ShapeDtypeStruct((width,), f32),
        ),
        in_specs=[away, whole, whole, whole, whole, whole, away, away],
        out_specs=(whole, whole, whole, whole),
        scratch_shapes=[
            pltpu.VMEM((rows, width), jnp.int32),
            pltpu.VMEM((count, width), bf16),
            pltpu.VMEM((4, count, width), bf16),
            pltpu.VMEM((2, rows, width), bf16),
            pltpu.VMEM((8, 2, width), f32),
            pltpu.VMEM((1, width), f32),
            pltpu.VMEM((4, count, rank), bf16),
            pltpu.VMEM((4, count, rank), bf16),
            pltpu.VMEM((4, count, rank), bf16),
            pltpu.VMEM((count, rank), f32),
            pltpu.VMEM((2, count, rows), f32),
            pltpu.VMEM((4, count, depth), bf16),
            pltpu.VMEM((4, 4, count // 4, depth), bf16),
            pltpu.VMEM((4, count // 4, depth), bf16),
            pltpu.VMEM((4, count // 4, depth), bf16),
            pltpu.VMEM((count, depth), bf16),
            pltpu.VMEM((4, rank, width), f32),
            pltpu.VMEM((2, rank, width), f32),
            pltpu.VMEM((3, rows, block_scales.shape[1]), bf16),
            pltpu.VMEM((rows, rank), bf16),
            pltpu.VMEM((8, rank // 8, depth), f32),
            pltpu.VMEM((8, rank // 8, depth), f32),
            pltpu.VMEM((8, rank // 8, depth), f32),
            pltpu.SemaphoreType.DMA((3,)),
            pltpu.SemaphoreType.DMA((72,)),
            pltpu.SemaphoreType.DMA((72,)),
        ],
        compiler_params=pltpu.CompilerParams(
            collective_id=0, has_side_effects=True, vmem_limit_bytes=58 * 1024 * 1024
        ),
    )(
        base_codes,
        block_scales.T,
        input_adapter_factor.T,
        output_adapter_factor,
        magnitude,
        inputs,
        grad_out,
        pre_scale,
    )
    return grad_inputs, first.T, second, grad_magnitude


def solution(mesh):
    fits = mesh.shape["dp"] == 8 and mesh.shape["tensor"] == 4
    body = on_device_fused if fits else on_device
    in_specs = (
        P("dp", "tensor"),
        P("dp", "tensor"),
        P(),
        P(None, "tensor"),
        P("tensor"),
        P("dp", "tensor"),
        P("dp", "tensor"),
        P("dp", "tensor"),
    )
    out_specs = (P("dp", "tensor"), P("tensor", None), P(None, "tensor"), P("tensor"))
    return jax.shard_map(
        body, mesh=mesh, in_specs=in_specs, out_specs=out_specs, check_vma=False
    )
```

```python
import jax
import jax.numpy as jnp
from jax import lax
from jax.experimental import pallas as pl
from jax.experimental.pallas import tpu as pltpu
from jax.sharding import PartitionSpec as P

adapter_scale_factor = 0.5


def on_device(
    base_codes,
    block_scales,
    input_adapter_factor,
    output_adapter_factor,
    magnitude,
    inputs,
    grad_out,
    pre_scale,
):
    f32, bf16 = jnp.float32, jnp.bfloat16
    row_count, columns = base_codes.shape
    tokens = grad_out.shape[0]
    dp = lax.axis_index("dp")
    block_size = columns // block_scales.shape[1]
    gathered = lax.all_gather(grad_out, "dp", axis=0, tiled=True)
    quarter_d = inputs.shape[1]
    adapter_part = lax.dynamic_slice_in_dim(
        input_adapter_factor, lax.axis_index("tensor") * quarter_d, quarter_d, 0
    )
    hidden_low = lax.psum(
        jnp.dot(inputs, adapter_part, preferred_element_type=f32).astype(bf16), "tensor"
    )
    hidden_all = lax.all_gather(hidden_low, "dp", axis=0, tiled=True)
    expanded = jnp.repeat(block_scales, block_size, axis=1)
    adapter_row_block = lax.dynamic_slice_in_dim(
        input_adapter_factor, dp * row_count, row_count, 0
    )
    merged = (
        (base_codes.astype(f32) - 7.5) * expanded
        + adapter_scale_factor
        * jnp.dot(adapter_row_block, output_adapter_factor, preferred_element_type=f32)
    ).astype(bf16)
    merged_f = merged.astype(f32)
    column_sums = jnp.sum(merged_f * merged_f, axis=0)
    magnitude_sums = jnp.sum(grad_out.astype(f32) * pre_scale.astype(f32), axis=0)
    column_sums, magnitude_sums = lax.psum((column_sums, magnitude_sums), "dp")
    col_norm = jnp.sqrt(column_sums + 1e-06)
    scaled = (gathered.astype(f32) * (magnitude / col_norm)).astype(bf16)
    partial_value = jnp.einsum("tf,rf->tr", scaled, merged, preferred_element_type=f32)
    exchanged = lax.all_to_all(
        partial_value.astype(bf16), "dp", split_axis=0, concat_axis=1, tiled=True
    )
    grad_inputs = lax.psum_scatter(exchanged, "tensor", scatter_dimension=1, tiled=True)
    own_scaled = lax.dynamic_slice_in_dim(scaled, dp * tokens, tokens, 0)
    back_low = lax.psum(
        jnp.einsum(
            "tf,rf->tr", own_scaled, output_adapter_factor, preferred_element_type=f32
        ).astype(bf16),
        "tensor",
    )
    input_gradient = lax.psum(
        adapter_scale_factor
        * jnp.einsum("td,tr->dr", inputs, back_low, preferred_element_type=f32),
        "dp",
    )
    output_gradient = adapter_scale_factor * jnp.einsum(
        "tr,tf->rf", hidden_all, scaled, preferred_element_type=f32
    )
    return (grad_inputs, input_gradient, output_gradient, magnitude_sums / col_norm)


MESH = pl.DeviceIdType.MESH
COLUMN_TILE = 512


def flip(bit, by):
    return bit + by - 2 * bit * by


def fused_kernel(
    codes_hbm,
    scales_ref,
    first_ref,
    second_ref,
    magnitude_ref,
    inputs_ref,
    grad_hbm,
    pre_hbm,
    out_ref,
    first_out,
    second_out,
    magnitude_out,
    codes,
    pre,
    tokens,
    weight,
    stats,
    factor,
    low_parts,
    low,
    back_parts,
    back_acc,
    scaled,
    product,
    shares,
    summed,
    returned,
    final,
    second_parts,
    second_pair,
    pieces,
    adapter_rows,
    first_split,
    first_recv,
    first_full,
    local_sem,
    send_sem,
    recv_sem,
):
    f32, bf16 = jnp.float32, jnp.bfloat16
    rows, width = codes.shape
    count = tokens.shape[1]
    half = count // 2
    group = rows // 2
    tile = COLUMN_TILE
    steps = width // tile
    rank = low.shape[2]
    block = width // scales_ref.shape[0]
    dp, z = lax.axis_index("dp"), lax.axis_index("tensor")
    core = lax.rem(dp, 2)
    x = lax.rem(dp // 2, 2)
    y = dp // 4
    z_low, z_high = lax.rem(z, 2), z // 2

    def plane(offset):
        return (
            flip(y, offset // 4) * 4 + flip(x, (offset // 2) % 2) * 2 + flip(core, offset % 2)
        )

    def stack(offset):
        return flip(z_high, offset // 2) * 2 + flip(z_low, offset % 2)

    used = [0]
    sent = []

    def remote(source, target, to, start=True):
        index = used[0]
        used[0] += 1
        copy = pltpu.make_async_remote_copy(
            src_ref=source,
            dst_ref=target,
            send_sem=send_sem.at[index],
            recv_sem=recv_sem.at[index],
            device_id=to,
            device_id_type=MESH,
        )
        copy.start()
        sent.append(copy)
        return copy

    def arrival(source, target, copy_index, to):
        return pltpu.make_async_remote_copy(
            src_ref=source,
            dst_ref=target,
            send_sem=send_sem.at[copy_index],
            recv_sem=recv_sem.at[copy_index],
            device_id=to,
            device_id_type=MESH,
        )

    def peer(offset):
        return {"dp": plane(offset), "tensor": z}

    def over(offset):
        return {"dp": dp, "tensor": stack(offset)}

    codes_copy = pltpu.make_async_copy(codes_hbm, codes, local_sem.at[0])
    pre_copy = pltpu.make_async_copy(pre_hbm, pre, local_sem.at[1])
    own_copy = pltpu.make_async_copy(grad_hbm, tokens.at[0], local_sem.at[2])
    codes_copy.start()
    pre_copy.start()
    own_copy.start()

    barrier = pltpu.get_barrier_semaphore()
    for offset in range(1, 8):
        pl.semaphore_signal(barrier, inc=1, device_id=peer(offset), device_id_type=MESH)
    for offset in range(1, 4):
        pl.semaphore_signal(barrier, inc=1, device_id=over(offset), device_id_type=MESH)
    pl.semaphore_wait(barrier, 10)

    lower, upper = pl.ds(0, half), pl.ds(half, half)
    from_x = [
        remote(grad_hbm.at[lower], tokens.at[1, lower], peer(2)),
    ]
    from_y = [
        remote(grad_hbm.at[upper], tokens.at[2, upper], peer(4)),
    ]
    from_x.append(remote(grad_hbm.at[upper], tokens.at[1, upper], peer(2)))
    from_y.append(remote(grad_hbm.at[lower], tokens.at[2, lower], peer(4)))

    depth = inputs_ref.shape[1]
    nt = (((1,), (1,)), ((), ()))
    tn = (((0,), (0,)), ((), ()))
    low_parts[0] = lax.dot_general(
        inputs_ref[...],
        first_ref[:, pl.ds(pl.multiple_of(z * depth, depth), depth)],
        nt,
        preferred_element_type=f32,
    ).astype(bf16)
    low_copies = [remote(low_parts.at[0], low_parts.at[r], over(r)) for r in range(1, 4)]

    own_rows = pl.ds(pl.multiple_of(dp * rows, rows), rows)
    adapter_rows[...] = jnp.transpose(first_ref[:, own_rows].astype(f32)).astype(bf16)
    scales = scales_ref[...]
    high = scales.astype(bf16).astype(f32)
    middle = (scales - high).astype(bf16).astype(f32)
    last = (scales - high) - middle
    pieces[...] = jnp.transpose(jnp.concatenate([high, middle, last], axis=0)).astype(bf16)
    codes_copy.wait()
    pre_copy.wait()
    own_copy.wait()

    def dequantize(step, carry):
        columns = pl.ds(pl.multiple_of(step * tile, tile), tile)
        shape = (scales_ref.shape[0], tile)
        place = lax.broadcasted_iota(jnp.int32, shape, 1) // block + step * (tile // block)
        chosen = jnp.where(lax.broadcasted_iota(jnp.int32, shape, 0) == place, 1.0, 0.0)
        spread = jnp.concatenate([chosen, chosen, chosen], axis=0).astype(bf16)
        expanded = jnp.dot(pieces[...], spread, preferred_element_type=f32)
        adapter = jnp.dot(adapter_rows[...], second_ref[:, columns], preferred_element_type=f32)
        merged = (
            (codes[:, columns].astype(f32) - 7.5) * expanded + adapter_scale_factor * adapter
        ).astype(bf16)
        weight[core * 2, :, columns] = merged[:group]
        weight[core * 2 + 1, :, columns] = merged[group:]
        merged_f = merged.astype(f32)
        stats[0, 0:1, columns] = jnp.sum(merged_f * merged_f, axis=0, keepdims=True)
        stats[0, 1:2, columns] = jnp.sum(
            tokens[0, :, columns].astype(f32) * pre[:, columns].astype(f32), axis=0, keepdims=True
        )
        return carry

    lax.fori_loop(0, steps, dequantize, 0)

    stats_copies = [remote(stats.at[0], stats.at[o], peer(o)) for o in range(1, 8)]
    weight_index = used[0]
    own_half, other_half = pl.ds(core * 2, 2), pl.ds(2 - core * 2, 2)
    remote(weight.at[own_half], weight.at[own_half], peer(1))
    weight_arrival = arrival(
        weight.at[own_half], weight.at[other_half], weight_index, peer(1)
    )

    for copy in low_copies:
        copy.wait_recv()
    low[0] = (
        (low_parts[0].astype(f32) + low_parts[1].astype(f32))
        + (low_parts[2].astype(f32) + low_parts[3].astype(f32))
    ).astype(bf16)
    plane_low = [remote(low.at[0], low.at[b], peer(2 * b)) for b in range(1, 4)]

    from_x[0].wait_recv()
    far_lower = remote(tokens.at[1, lower], tokens.at[3, lower], peer(4))
    from_y[0].wait_recv()
    far_upper = remote(tokens.at[2, upper], tokens.at[3, upper], peer(2))

    for copy in stats_copies:
        copy.wait_recv()
    total = ((stats[0] + stats[1]) + (stats[2] + stats[3])) + (
        (stats[4] + stats[5]) + (stats[6] + stats[7])
    )
    norm = jnp.sqrt(total[0:1, :] + 1e-06)
    factor[...] = magnitude_ref[...].reshape(1, width) / norm
    magnitude_out[...] = (total[1:2, :] / norm).reshape(width)

    weight_arrival.wait_recv()

    part = count // 4

    def part_rows(to_z):
        return pl.ds(pl.multiple_of(to_z * part, part), part)

    full = pl.ds(0, depth)
    groups = [pl.ds(n * group, group) for n in range(4)]

    def send_shares(which, columns):
        return [
            remote(
                product.at[which, part_rows(stack(r)), columns],
                shares.at[which, r, :, columns],
                over(r),
            )
            for r in range(1, 4)
        ]

    def sum_shares(which, copies, columns):
        for copy in copies:
            copy.wait_recv()
        target = returned if which == 0 else summed
        target[which, :, columns] = (
            (product[which, part_rows(z), columns].astype(f32) + shares[which, 1, :, columns].astype(f32))
            + (shares[which, 2, :, columns].astype(f32) + shares[which, 3, :, columns].astype(f32))
        ).astype(bf16)
        if which == 0:
            return None
        return remote(
            summed.at[which, :, columns], returned.at[which, :, columns], peer(2 * which)
        )

    final_sends = []
    final_index = used[0]
    used[0] += 16

    def final_copy(which, slot, n, target_rows, to):
        return pltpu.make_async_remote_copy(
            src_ref=returned.at[which, :, groups[n]],
            dst_ref=final.at[target_rows, groups[n]],
            send_sem=send_sem.at[final_index + which * 4 + n],
            recv_sem=recv_sem.at[final_index + slot * 4 + n],
            device_id=to,
            device_id_type=MESH,
        )

    def send_final(which, pieces_sent=range(4)):
        quarter_high, quarter_low = flip(y, which // 2), flip(x, which % 2)
        to_z = quarter_high * 2 + quarter_low
        slot = flip(quarter_high, z_high) * 2 + flip(quarter_low, z_low)
        for n in pieces_sent:
            copy = final_copy(which, slot, n, part_rows(z), {"dp": dp, "tensor": to_z})

            @pl.when(to_z != z)
            def _(copy=copy):
                copy.start()

            @pl.when(to_z == z)
            def _(n=n):
                final[part_rows(z), groups[n]] = returned[which, :, groups[n]]

            final_sends.append((copy, to_z))

    def scale_tokens(which):
        def body(step, carry):
            columns = pl.ds(pl.multiple_of(step * tile, tile), tile)
            scaled[:, columns] = (
                tokens[which, :, columns].astype(f32) * factor[:, columns]
            ).astype(bf16)
            return carry

        lax.fori_loop(0, steps, body, 0)

    def multiply_group(which, n):
        product[which, :, groups[n]] = lax.dot_general(
            scaled[...], weight[n], nt, preferred_element_type=f32
        ).astype(bf16)

    def second_product(which):
        if which == 0:
            back_acc[...] = jnp.zeros_like(back_acc)

        def body(step, carry):
            columns = pl.ds(pl.multiple_of(step * tile, tile), tile)
            second_parts[which, :, columns] = lax.dot_general(
                low[which], scaled[:, columns], tn, preferred_element_type=f32
            )
            if which == 0:
                back_acc[...] += lax.dot_general(
                    scaled[:, columns], second_ref[:, columns], nt, preferred_element_type=f32
                )
            return carry

        lax.fori_loop(0, steps, body, 0)

    def multiply(which):
        scale_tokens(which)
        for n in range(4):
            multiply_group(which, n)
        copies = send_shares(which, full)
        second_product(which)
        return copies

    shares_0 = multiply(0)
    back_parts[0] = back_acc[...].astype(bf16)
    back_copies = [remote(back_parts.at[0], back_parts.at[r], over(r)) for r in range(1, 4)]

    from_x[1].wait_recv()
    plane_low[0].wait_recv()
    shares_1 = multiply(1)
    sum_shares(0, shares_0, full)
    send_final(0)

    from_y[1].wait_recv()
    plane_low[1].wait_recv()
    shares_2 = multiply(2)
    return_1 = sum_shares(1, shares_1, full)

    for copy in back_copies:
        copy.wait_recv()
    back = (
        (back_parts[0].astype(f32) + back_parts[1].astype(f32))
        + (back_parts[2].astype(f32) + back_parts[3].astype(f32))
    ).astype(bf16)
    slices = first_split.shape[0]
    piece = rank // slices
    gradient = adapter_scale_factor * lax.dot_general(
        back, inputs_ref[...], tn, preferred_element_type=f32
    )
    for index in range(slices):
        first_split[index] = gradient[index * piece : (index + 1) * piece, :]

    return_2 = sum_shares(2, shares_2, full)
    return_1.wait_recv()
    send_final(1)

    far_lower.wait_recv()
    far_upper.wait_recv()
    plane_low[2].wait_recv()
    scale_tokens(3)
    shares_3 = []
    for n in range(4):
        multiply_group(3, n)
        shares_3.append(send_shares(3, groups[n]))
    return_2.wait_recv()
    send_final(2)
    returns_3 = [sum_shares(3, shares_3[n], groups[n]) for n in range(2)]
    second_product(3)
    returns_3 += [sum_shares(3, shares_3[n], groups[n]) for n in range(2, 4)]
    first_copies = [
        remote(first_split.at[plane(o)], first_recv.at[o], peer(o)) for o in range(1, 8)
    ]
    second_pair[0] = (second_parts[0] + second_parts[1]) + (second_parts[2] + second_parts[3])
    pair_copy = remote(second_pair.at[0], second_pair.at[1], peer(1))
    for n in range(4):
        returns_3[n].wait_recv()
        send_final(3, (n,))

    for copy in first_copies:
        copy.wait_recv()
    first_recv[0] = first_split[dp]
    first_full[dp] = (
        (first_recv[0] + first_recv[1]) + (first_recv[2] + first_recv[3])
    ) + ((first_recv[4] + first_recv[5]) + (first_recv[6] + first_recv[7]))
    first_index = used[0]
    for o in range(1, 8):
        remote(first_full.at[dp], first_full.at[dp], peer(o))

    pair_copy.wait_recv()
    second_out[...] = adapter_scale_factor * (second_pair[0] + second_pair[1])
    for o in range(1, 8):
        arrival(
            first_full.at[dp], first_full.at[plane(o)], first_index + o - 1, peer(o)
        ).wait_recv()
    first_out[...] = first_full[...].reshape(rank, depth)

    for n in range(4):
        for slot in range(1, 4):
            final_copy(slot, slot, n, part_rows(stack(slot)), over(slot)).wait_recv()
    out_ref[...] = final[...]

    for copy in sent:
        copy.wait_send()
    for copy, to_z in final_sends:

        @pl.when(to_z != z)
        def _(copy=copy):
            copy.wait_send()


def on_device_fused(
    base_codes,
    block_scales,
    input_adapter_factor,
    output_adapter_factor,
    magnitude,
    inputs,
    grad_out,
    pre_scale,
):
    f32, bf16 = jnp.float32, jnp.bfloat16
    rows, width = base_codes.shape
    count, depth = inputs.shape
    rank = input_adapter_factor.shape[1]
    whole = pl.BlockSpec(memory_space=pltpu.VMEM)
    away = pl.BlockSpec(memory_space=pl.ANY)
    grad_inputs, first, second, grad_magnitude = pl.pallas_call(
        fused_kernel,
        out_shape=(
            jax.ShapeDtypeStruct((count, depth), bf16),
            jax.ShapeDtypeStruct((rank, depth), f32),
            jax.ShapeDtypeStruct((rank, width), f32),
            jax.ShapeDtypeStruct((width,), f32),
        ),
        in_specs=[away, whole, whole, whole, whole, whole, away, away],
        out_specs=(whole, whole, whole, whole),
        scratch_shapes=[
            pltpu.VMEM((rows, width), jnp.int32),
            pltpu.VMEM((count, width), bf16),
            pltpu.VMEM((4, count, width), bf16),
            pltpu.VMEM((4, rows // 2, width), bf16),
            pltpu.VMEM((8, 2, width), f32),
            pltpu.VMEM((1, width), f32),
            pltpu.VMEM((4, count, rank), bf16),
            pltpu.VMEM((4, count, rank), bf16),
            pltpu.VMEM((4, count, rank), bf16),
            pltpu.VMEM((count, rank), f32),
            pltpu.VMEM((count, width), bf16),
            pltpu.VMEM((4, count, depth), bf16),
            pltpu.VMEM((4, 4, count // 4, depth), bf16),
            pltpu.VMEM((4, count // 4, depth), bf16),
            pltpu.VMEM((4, count // 4, depth), bf16),
            pltpu.VMEM((count, depth), bf16),
            pltpu.VMEM((4, rank, width), f32),
            pltpu.VMEM((2, rank, width), f32),
            pltpu.VMEM((rows, 3 * block_scales.shape[1]), bf16),
            pltpu.VMEM((rows, rank), bf16),
            pltpu.VMEM((8, rank // 8, depth), f32),
            pltpu.VMEM((8, rank // 8, depth), f32),
            pltpu.VMEM((8, rank // 8, depth), f32),
            pltpu.SemaphoreType.DMA((3,)),
            pltpu.SemaphoreType.DMA((96,)),
            pltpu.SemaphoreType.DMA((96,)),
        ],
        compiler_params=pltpu.CompilerParams(
            collective_id=0, has_side_effects=True, vmem_limit_bytes=58 * 1024 * 1024
        ),
    )(
        base_codes,
        block_scales.T,
        input_adapter_factor.T,
        output_adapter_factor,
        magnitude,
        inputs,
        grad_out,
        pre_scale,
    )
    return grad_inputs, first.T, second, grad_magnitude


def solution(mesh):
    fits = mesh.shape["dp"] == 8 and mesh.shape["tensor"] == 4
    body = on_device_fused if fits else on_device
    in_specs = (
        P("dp", "tensor"),
        P("dp", "tensor"),
        P(),
        P(None, "tensor"),
        P("tensor"),
        P("dp", "tensor"),
        P("dp", "tensor"),
        P("dp", "tensor"),
    )
    out_specs = (P("dp", "tensor"), P("tensor", None), P(None, "tensor"), P("tensor"))
    return jax.shard_map(
        body, mesh=mesh, in_specs=in_specs, out_specs=out_specs, check_vma=False
    )
```

```python
import jax
import jax.numpy as jnp
from jax import lax
from jax.experimental import pallas as pl
from jax.experimental.pallas import tpu as pltpu
from jax.sharding import PartitionSpec as P

adapter_scale_factor = 0.5


def on_device(
    base_codes,
    block_scales,
    input_adapter_factor,
    output_adapter_factor,
    magnitude,
    inputs,
    grad_out,
    pre_scale,
):
    f32, bf16 = jnp.float32, jnp.bfloat16
    row_count, columns = base_codes.shape
    tokens = grad_out.shape[0]
    dp = lax.axis_index("dp")
    block_size = columns // block_scales.shape[1]
    gathered = lax.all_gather(grad_out, "dp", axis=0, tiled=True)
    quarter_d = inputs.shape[1]
    adapter_part = lax.dynamic_slice_in_dim(
        input_adapter_factor, lax.axis_index("tensor") * quarter_d, quarter_d, 0
    )
    hidden_low = lax.psum(
        jnp.dot(inputs, adapter_part, preferred_element_type=f32).astype(bf16), "tensor"
    )
    hidden_all = lax.all_gather(hidden_low, "dp", axis=0, tiled=True)
    expanded = jnp.repeat(block_scales, block_size, axis=1)
    adapter_row_block = lax.dynamic_slice_in_dim(
        input_adapter_factor, dp * row_count, row_count, 0
    )
    merged = (
        (base_codes.astype(f32) - 7.5) * expanded
        + adapter_scale_factor
        * jnp.dot(adapter_row_block, output_adapter_factor, preferred_element_type=f32)
    ).astype(bf16)
    merged_f = merged.astype(f32)
    column_sums = jnp.sum(merged_f * merged_f, axis=0)
    magnitude_sums = jnp.sum(grad_out.astype(f32) * pre_scale.astype(f32), axis=0)
    column_sums, magnitude_sums = lax.psum((column_sums, magnitude_sums), "dp")
    col_norm = jnp.sqrt(column_sums + 1e-06)
    scaled = (gathered.astype(f32) * (magnitude / col_norm)).astype(bf16)
    partial_value = jnp.einsum("tf,rf->tr", scaled, merged, preferred_element_type=f32)
    exchanged = lax.all_to_all(
        partial_value.astype(bf16), "dp", split_axis=0, concat_axis=1, tiled=True
    )
    grad_inputs = lax.psum_scatter(exchanged, "tensor", scatter_dimension=1, tiled=True)
    own_scaled = lax.dynamic_slice_in_dim(scaled, dp * tokens, tokens, 0)
    back_low = lax.psum(
        jnp.einsum(
            "tf,rf->tr", own_scaled, output_adapter_factor, preferred_element_type=f32
        ).astype(bf16),
        "tensor",
    )
    input_gradient = lax.psum(
        adapter_scale_factor
        * jnp.einsum("td,tr->dr", inputs, back_low, preferred_element_type=f32),
        "dp",
    )
    output_gradient = adapter_scale_factor * jnp.einsum(
        "tr,tf->rf", hidden_all, scaled, preferred_element_type=f32
    )
    return (grad_inputs, input_gradient, output_gradient, magnitude_sums / col_norm)


MESH = pl.DeviceIdType.MESH
COLUMN_TILE = 512


def flip(bit, by):
    return bit + by - 2 * bit * by


def fused_kernel(
    codes_hbm,
    scales_ref,
    first_ref,
    second_ref,
    magnitude_ref,
    inputs_ref,
    grad_hbm,
    pre_hbm,
    out_ref,
    first_out,
    second_out,
    magnitude_out,
    codes,
    pre,
    tokens,
    weight,
    stats,
    factor,
    low_parts,
    low,
    back_parts,
    back_acc,
    scaled,
    product,
    shares,
    summed,
    returned,
    final,
    second_parts,
    second_pair,
    pieces,
    adapter_rows,
    first_split,
    first_recv,
    first_full,
    local_sem,
    send_sem,
    recv_sem,
):
    f32, bf16 = jnp.float32, jnp.bfloat16
    rows, width = codes.shape
    count = tokens.shape[1]
    half = count // 2
    group = rows // 2
    tile = COLUMN_TILE
    steps = width // tile
    rank = low.shape[2]
    block = width // scales_ref.shape[0]
    dp, z = lax.axis_index("dp"), lax.axis_index("tensor")
    core = lax.rem(dp, 2)
    x = lax.rem(dp // 2, 2)
    y = dp // 4
    z_low, z_high = lax.rem(z, 2), z // 2

    def plane(offset):
        return (
            flip(y, offset // 4) * 4 + flip(x, (offset // 2) % 2) * 2 + flip(core, offset % 2)
        )

    def stack(offset):
        return flip(z_high, offset // 2) * 2 + flip(z_low, offset % 2)

    used = [0]
    sent = []

    def remote(source, target, to, start=True):
        index = used[0]
        used[0] += 1
        copy = pltpu.make_async_remote_copy(
            src_ref=source,
            dst_ref=target,
            send_sem=send_sem.at[index],
            recv_sem=recv_sem.at[index],
            device_id=to,
            device_id_type=MESH,
        )
        copy.start()
        sent.append(copy)
        return copy

    def arrival(source, target, copy_index, to):
        return pltpu.make_async_remote_copy(
            src_ref=source,
            dst_ref=target,
            send_sem=send_sem.at[copy_index],
            recv_sem=recv_sem.at[copy_index],
            device_id=to,
            device_id_type=MESH,
        )

    def peer(offset):
        return {"dp": plane(offset), "tensor": z}

    def over(offset):
        return {"dp": dp, "tensor": stack(offset)}

    codes_copy = pltpu.make_async_copy(codes_hbm, codes, local_sem.at[0])
    pre_copy = pltpu.make_async_copy(pre_hbm, pre, local_sem.at[1])
    own_copy = pltpu.make_async_copy(grad_hbm, tokens.at[0], local_sem.at[2])
    codes_copy.start()
    pre_copy.start()
    own_copy.start()

    barrier = pltpu.get_barrier_semaphore()
    for offset in range(1, 8):
        pl.semaphore_signal(barrier, inc=1, device_id=peer(offset), device_id_type=MESH)
    for offset in range(1, 4):
        pl.semaphore_signal(barrier, inc=1, device_id=over(offset), device_id_type=MESH)
    pl.semaphore_wait(barrier, 10)

    lower, upper = pl.ds(0, half), pl.ds(half, half)
    from_x = [
        remote(grad_hbm.at[lower], tokens.at[1, lower], peer(2)),
    ]
    from_y = [
        remote(grad_hbm.at[upper], tokens.at[2, upper], peer(4)),
    ]

    depth = inputs_ref.shape[1]
    nt = (((1,), (1,)), ((), ()))
    tn = (((0,), (0,)), ((), ()))
    low_parts[0] = lax.dot_general(
        inputs_ref[...],
        first_ref[:, pl.ds(pl.multiple_of(z * depth, depth), depth)],
        nt,
        preferred_element_type=f32,
    ).astype(bf16)
    low_copies = [remote(low_parts.at[0], low_parts.at[r], over(r)) for r in range(1, 4)]

    own_rows = pl.ds(pl.multiple_of(dp * rows, rows), rows)
    adapter_rows[...] = jnp.transpose(first_ref[:, own_rows].astype(f32)).astype(bf16)
    scales = scales_ref[...]
    high = scales.astype(bf16).astype(f32)
    middle = (scales - high).astype(bf16).astype(f32)
    last = (scales - high) - middle
    pieces[...] = jnp.transpose(jnp.concatenate([high, middle, last], axis=0)).astype(bf16)
    codes_copy.wait()
    pre_copy.wait()
    own_copy.wait()

    def dequantize(step, carry):
        columns = pl.ds(pl.multiple_of(step * tile, tile), tile)
        shape = (scales_ref.shape[0], tile)
        place = lax.broadcasted_iota(jnp.int32, shape, 1) // block + step * (tile // block)
        chosen = jnp.where(lax.broadcasted_iota(jnp.int32, shape, 0) == place, 1.0, 0.0)
        spread = jnp.concatenate([chosen, chosen, chosen], axis=0).astype(bf16)
        expanded = jnp.dot(pieces[...], spread, preferred_element_type=f32)
        adapter = jnp.dot(adapter_rows[...], second_ref[:, columns], preferred_element_type=f32)
        merged = (
            (codes[:, columns].astype(f32) - 7.5) * expanded + adapter_scale_factor * adapter
        ).astype(bf16)
        weight[core * 2, :, columns] = merged[:group]
        weight[core * 2 + 1, :, columns] = merged[group:]
        merged_f = merged.astype(f32)
        stats[0, 0:1, columns] = jnp.sum(merged_f * merged_f, axis=0, keepdims=True)
        stats[0, 1:2, columns] = jnp.sum(
            tokens[0, :, columns].astype(f32) * pre[:, columns].astype(f32), axis=0, keepdims=True
        )
        return carry

    lax.fori_loop(0, steps, dequantize, 0)

    stats_copies = [remote(stats.at[0], stats.at[o], peer(o)) for o in range(1, 8)]
    weight_index = used[0]
    own_half, other_half = pl.ds(core * 2, 2), pl.ds(2 - core * 2, 2)
    remote(weight.at[own_half], weight.at[own_half], peer(1))
    weight_arrival = arrival(
        weight.at[own_half], weight.at[other_half], weight_index, peer(1)
    )
    from_x.append(remote(grad_hbm.at[upper], tokens.at[1, upper], peer(2)))
    from_y.append(remote(grad_hbm.at[lower], tokens.at[2, lower], peer(4)))

    for copy in low_copies:
        copy.wait_recv()
    low[0] = (
        (low_parts[0].astype(f32) + low_parts[1].astype(f32))
        + (low_parts[2].astype(f32) + low_parts[3].astype(f32))
    ).astype(bf16)
    plane_low = [remote(low.at[0], low.at[b], peer(2 * b)) for b in range(1, 4)]

    for copy in stats_copies:
        copy.wait_recv()
    total = ((stats[0] + stats[1]) + (stats[2] + stats[3])) + (
        (stats[4] + stats[5]) + (stats[6] + stats[7])
    )
    norm = jnp.sqrt(total[0:1, :] + 1e-06)
    factor[...] = magnitude_ref[...].reshape(1, width) / norm
    magnitude_out[...] = (total[1:2, :] / norm).reshape(width)

    part = count // 4

    def part_rows(to_z):
        return pl.ds(pl.multiple_of(to_z * part, part), part)

    full = pl.ds(0, depth)
    groups = [pl.ds(n * group, group) for n in range(4)]

    def send_shares(which, columns):
        return [
            remote(
                product.at[which, part_rows(stack(r)), columns],
                shares.at[which, r, :, columns],
                over(r),
            )
            for r in range(1, 4)
        ]

    def sum_shares(which, copies, columns):
        for copy in copies:
            copy.wait_recv()
        target = returned if which == 0 else summed
        slot, to = which, peer(2 * which)
        if which in (1, 2):
            slot = 1 + z_high if which == 1 else 2 - z_high
            to_y, to_x = flip(y, slot - 1), flip(x, 2 - slot)
            to = {"dp": to_y * 4 + to_x * 2 + core, "tensor": z}
        target[which, :, columns] = (
            (product[which, part_rows(z), columns].astype(f32) + shares[which, 1, :, columns].astype(f32))
            + (shares[which, 2, :, columns].astype(f32) + shares[which, 3, :, columns].astype(f32))
        ).astype(bf16)
        if which == 0:
            return None
        return remote(
            summed.at[which, :, columns], returned.at[slot, :, columns], to
        )

    final_sends = []
    final_index = used[0]
    used[0] += 16

    def final_copy(which, tag, slot, n, target_rows, to):
        return pltpu.make_async_remote_copy(
            src_ref=returned.at[which, :, groups[n]],
            dst_ref=final.at[target_rows, groups[n]],
            send_sem=send_sem.at[final_index + tag * 4 + n],
            recv_sem=recv_sem.at[final_index + slot * 4 + n],
            device_id=to,
            device_id_type=MESH,
        )

    def send_final(tag, pieces_sent=range(4)):
        which, over_y, over_x = tag, tag // 2, tag % 2
        if tag in (1, 2):
            which = 1 + z_high if tag == 1 else 2 - z_high
            over_y, over_x = which - 1, 2 - which
        quarter_high, quarter_low = flip(y, over_y), flip(x, over_x)
        to_z = quarter_high * 2 + quarter_low
        slot = flip(quarter_high, z_high) * 2 + flip(quarter_low, z_low)
        for n in pieces_sent:
            copy = final_copy(which, tag, slot, n, part_rows(z), {"dp": dp, "tensor": to_z})

            @pl.when(to_z != z)
            def _(copy=copy):
                copy.start()

            @pl.when(to_z == z)
            def _(n=n):
                final[part_rows(z), groups[n]] = returned[which, :, groups[n]]

            final_sends.append((copy, to_z))

    def scale_tokens(lower_block, upper_block):
        def body(step, carry):
            columns = pl.ds(pl.multiple_of(step * tile, tile), tile)
            for which, part in ((lower_block, lower), (upper_block, upper)):
                scaled[part, columns] = (
                    tokens[which, part, columns].astype(f32) * factor[:, columns]
                ).astype(bf16)
            return carry

        lax.fori_loop(0, steps, body, 0)

    def multiply_group(which, n):
        columns = pl.ds(pl.multiple_of(n * group, group), group)
        product[which, :, columns] = lax.dot_general(
            scaled[...], weight[n], nt, preferred_element_type=f32
        ).astype(bf16)

    def second_product(which):
        if which == 0:
            back_acc[...] = jnp.zeros_like(back_acc)

        def body(step, carry):
            columns = pl.ds(pl.multiple_of(step * tile, tile), tile)
            values = (tokens[which, :, columns].astype(f32) * factor[:, columns]).astype(bf16)
            second_parts[which, :, columns] = lax.dot_general(
                low[which], values, tn, preferred_element_type=f32
            )
            if which == 0:
                back_acc[...] += lax.dot_general(
                    values, second_ref[:, columns], nt, preferred_element_type=f32
                )
            return carry

        lax.fori_loop(0, steps, body, 0)

    scale_tokens(0, 0)
    for n in range(2):
        multiply_group(0, core * 2 + n)
    weight_arrival.wait_recv()
    for n in range(2):
        multiply_group(0, 2 - core * 2 + n)
    shares_0 = send_shares(0, full)

    from_x[0].wait_recv()
    far_lower = remote(tokens.at[1, lower], tokens.at[3, lower], peer(4))
    from_y[0].wait_recv()
    far_upper = remote(tokens.at[2, upper], tokens.at[3, upper], peer(2))

    scale_tokens(1, 2)
    for n in range(4):
        multiply_group(1, n)
    shares_1 = send_shares(1, full)

    second_product(0)
    back_parts[0] = back_acc[...].astype(bf16)
    back_copies = [remote(back_parts.at[0], back_parts.at[r], over(r)) for r in range(1, 4)]
    sum_shares(0, shares_0, full)
    send_final(0)

    from_x[1].wait_recv()
    from_y[1].wait_recv()
    scale_tokens(2, 1)
    for n in range(4):
        multiply_group(2, n)
    shares_2 = send_shares(2, full)
    return_1 = sum_shares(1, shares_1, full)

    plane_low[0].wait_recv()
    second_product(1)
    plane_low[1].wait_recv()
    second_product(2)

    for copy in back_copies:
        copy.wait_recv()
    back = (
        (back_parts[0].astype(f32) + back_parts[1].astype(f32))
        + (back_parts[2].astype(f32) + back_parts[3].astype(f32))
    ).astype(bf16)
    slices = first_split.shape[0]
    piece = rank // slices
    gradient = adapter_scale_factor * lax.dot_general(
        back, inputs_ref[...], tn, preferred_element_type=f32
    )
    for index in range(slices):
        first_split[index] = gradient[index * piece : (index + 1) * piece, :]

    return_1.wait_recv()
    send_final(1)
    return_2 = sum_shares(2, shares_2, full)

    far_lower.wait_recv()
    far_upper.wait_recv()
    plane_low[2].wait_recv()
    scale_tokens(3, 3)
    shares_3 = []
    for n in range(4):
        multiply_group(3, n)
        shares_3.append(send_shares(3, groups[n]))
    return_2.wait_recv()
    send_final(2)
    returns_3 = [sum_shares(3, shares_3[n], groups[n]) for n in range(2)]
    second_product(3)
    returns_3 += [sum_shares(3, shares_3[n], groups[n]) for n in range(2, 4)]
    first_copies = [
        remote(first_split.at[plane(o)], first_recv.at[o], peer(o)) for o in range(1, 8)
    ]
    second_pair[0] = (second_parts[0] + second_parts[1]) + (second_parts[2] + second_parts[3])
    pair_copy = remote(second_pair.at[0], second_pair.at[1], peer(1))
    for n in range(4):
        returns_3[n].wait_recv()
        send_final(3, (n,))

    for copy in first_copies:
        copy.wait_recv()
    first_recv[0] = first_split[dp]
    first_full[dp] = (
        (first_recv[0] + first_recv[1]) + (first_recv[2] + first_recv[3])
    ) + ((first_recv[4] + first_recv[5]) + (first_recv[6] + first_recv[7]))
    first_index = used[0]
    for o in range(1, 8):
        remote(first_full.at[dp], first_full.at[dp], peer(o))

    pair_copy.wait_recv()
    second_out[...] = adapter_scale_factor * (second_pair[0] + second_pair[1])
    for o in range(1, 8):
        arrival(
            first_full.at[dp], first_full.at[plane(o)], first_index + o - 1, peer(o)
        ).wait_recv()
    first_out[...] = first_full[...].reshape(rank, depth)

    for n in range(4):
        for slot in range(1, 4):
            final_copy(slot, slot, slot, n, part_rows(stack(slot)), over(slot)).wait_recv()
    out_ref[...] = final[...]

    for copy in sent:
        copy.wait_send()
    for copy, to_z in final_sends:

        @pl.when(to_z != z)
        def _(copy=copy):
            copy.wait_send()


def on_device_fused(
    base_codes,
    block_scales,
    input_adapter_factor,
    output_adapter_factor,
    magnitude,
    inputs,
    grad_out,
    pre_scale,
):
    f32, bf16 = jnp.float32, jnp.bfloat16
    rows, width = base_codes.shape
    count, depth = inputs.shape
    rank = input_adapter_factor.shape[1]
    whole = pl.BlockSpec(memory_space=pltpu.VMEM)
    away = pl.BlockSpec(memory_space=pl.ANY)
    grad_inputs, first, second, grad_magnitude = pl.pallas_call(
        fused_kernel,
        out_shape=(
            jax.ShapeDtypeStruct((count, depth), bf16),
            jax.ShapeDtypeStruct((rank, depth), f32),
            jax.ShapeDtypeStruct((rank, width), f32),
            jax.ShapeDtypeStruct((width,), f32),
        ),
        in_specs=[away, whole, whole, whole, whole, whole, away, away],
        out_specs=(whole, whole, whole, whole),
        scratch_shapes=[
            pltpu.VMEM((rows, width), jnp.int32),
            pltpu.VMEM((count, width), bf16),
            pltpu.VMEM((4, count, width), bf16),
            pltpu.VMEM((4, rows // 2, width), bf16),
            pltpu.VMEM((8, 2, width), f32),
            pltpu.VMEM((1, width), f32),
            pltpu.VMEM((4, count, rank), bf16),
            pltpu.VMEM((4, count, rank), bf16),
            pltpu.VMEM((4, count, rank), bf16),
            pltpu.VMEM((count, rank), f32),
            pltpu.VMEM((count, width), bf16),
            pltpu.VMEM((4, count, depth), bf16),
            pltpu.VMEM((4, 4, count // 4, depth), bf16),
            pltpu.VMEM((4, count // 4, depth), bf16),
            pltpu.VMEM((4, count // 4, depth), bf16),
            pltpu.VMEM((count, depth), bf16),
            pltpu.VMEM((4, rank, width), f32),
            pltpu.VMEM((2, rank, width), f32),
            pltpu.VMEM((rows, 3 * block_scales.shape[1]), bf16),
            pltpu.VMEM((rows, rank), bf16),
            pltpu.VMEM((8, rank // 8, depth), f32),
            pltpu.VMEM((8, rank // 8, depth), f32),
            pltpu.VMEM((8, rank // 8, depth), f32),
            pltpu.SemaphoreType.DMA((3,)),
            pltpu.SemaphoreType.DMA((96,)),
            pltpu.SemaphoreType.DMA((96,)),
        ],
        compiler_params=pltpu.CompilerParams(
            collective_id=0, has_side_effects=True, vmem_limit_bytes=58 * 1024 * 1024
        ),
    )(
        base_codes,
        block_scales.T,
        input_adapter_factor.T,
        output_adapter_factor,
        magnitude,
        inputs,
        grad_out,
        pre_scale,
    )
    return grad_inputs, first.T, second, grad_magnitude


def solution(mesh):
    fits = mesh.shape["dp"] == 8 and mesh.shape["tensor"] == 4
    body = on_device_fused if fits else on_device
    in_specs = (
        P("dp", "tensor"),
        P("dp", "tensor"),
        P(),
        P(None, "tensor"),
        P("tensor"),
        P("dp", "tensor"),
        P("dp", "tensor"),
        P("dp", "tensor"),
    )
    out_specs = (P("dp", "tensor"), P("tensor", None), P(None, "tensor"), P("tensor"))
    return jax.shard_map(
        body, mesh=mesh, in_specs=in_specs, out_specs=out_specs, check_vma=False
    )
```

```python
import jax
import jax.numpy as jnp
from jax import lax
from jax.experimental import pallas as pl
from jax.experimental.pallas import tpu as pltpu
from jax.sharding import PartitionSpec as P

adapter_scale_factor = 0.5


def on_device(
    base_codes,
    block_scales,
    input_adapter_factor,
    output_adapter_factor,
    magnitude,
    inputs,
    grad_out,
    pre_scale,
):
    f32, bf16 = jnp.float32, jnp.bfloat16
    row_count, columns = base_codes.shape
    tokens = grad_out.shape[0]
    dp = lax.axis_index("dp")
    block_size = columns // block_scales.shape[1]
    gathered = lax.all_gather(grad_out, "dp", axis=0, tiled=True)
    quarter_d = inputs.shape[1]
    adapter_part = lax.dynamic_slice_in_dim(
        input_adapter_factor, lax.axis_index("tensor") * quarter_d, quarter_d, 0
    )
    hidden_low = lax.psum(
        jnp.dot(inputs, adapter_part, preferred_element_type=f32).astype(bf16), "tensor"
    )
    hidden_all = lax.all_gather(hidden_low, "dp", axis=0, tiled=True)
    expanded = jnp.repeat(block_scales, block_size, axis=1)
    adapter_row_block = lax.dynamic_slice_in_dim(
        input_adapter_factor, dp * row_count, row_count, 0
    )
    merged = (
        (base_codes.astype(f32) - 7.5) * expanded
        + adapter_scale_factor
        * jnp.dot(adapter_row_block, output_adapter_factor, preferred_element_type=f32)
    ).astype(bf16)
    merged_f = merged.astype(f32)
    column_sums = jnp.sum(merged_f * merged_f, axis=0)
    magnitude_sums = jnp.sum(grad_out.astype(f32) * pre_scale.astype(f32), axis=0)
    column_sums, magnitude_sums = lax.psum((column_sums, magnitude_sums), "dp")
    col_norm = jnp.sqrt(column_sums + 1e-06)
    scaled = (gathered.astype(f32) * (magnitude / col_norm)).astype(bf16)
    partial_value = jnp.einsum("tf,rf->tr", scaled, merged, preferred_element_type=f32)
    exchanged = lax.all_to_all(
        partial_value.astype(bf16), "dp", split_axis=0, concat_axis=1, tiled=True
    )
    grad_inputs = lax.psum_scatter(exchanged, "tensor", scatter_dimension=1, tiled=True)
    own_scaled = lax.dynamic_slice_in_dim(scaled, dp * tokens, tokens, 0)
    back_low = lax.psum(
        jnp.einsum(
            "tf,rf->tr", own_scaled, output_adapter_factor, preferred_element_type=f32
        ).astype(bf16),
        "tensor",
    )
    input_gradient = lax.psum(
        adapter_scale_factor
        * jnp.einsum("td,tr->dr", inputs, back_low, preferred_element_type=f32),
        "dp",
    )
    output_gradient = adapter_scale_factor * jnp.einsum(
        "tr,tf->rf", hidden_all, scaled, preferred_element_type=f32
    )
    return (grad_inputs, input_gradient, output_gradient, magnitude_sums / col_norm)


MESH = pl.DeviceIdType.MESH
COLUMN_TILE = 512


def flip(bit, by):
    return bit + by - 2 * bit * by


def fused_kernel(
    codes_hbm,
    scales_ref,
    first_ref,
    second_ref,
    magnitude_ref,
    inputs_ref,
    grad_hbm,
    pre_hbm,
    out_ref,
    first_out,
    second_out,
    magnitude_out,
    codes,
    pre,
    tokens,
    weight,
    stats,
    factor,
    low_parts,
    low,
    back_parts,
    back_acc,
    scaled,
    product,
    shares,
    summed,
    returned,
    final,
    second_parts,
    second_pair,
    pieces,
    adapter_rows,
    first_split,
    first_recv,
    first_full,
    local_sem,
    send_sem,
    recv_sem,
):
    f32, bf16 = jnp.float32, jnp.bfloat16
    rows, width = codes.shape
    count = tokens.shape[1]
    half = count // 2
    group = rows // 2
    tile = COLUMN_TILE
    steps = width // tile
    rank = low.shape[2]
    block = width // scales_ref.shape[0]
    dp, z = lax.axis_index("dp"), lax.axis_index("tensor")
    core = lax.rem(dp, 2)
    x = lax.rem(dp // 2, 2)
    y = dp // 4
    z_low, z_high = lax.rem(z, 2), z // 2

    def plane(offset):
        return (
            flip(y, offset // 4) * 4 + flip(x, (offset // 2) % 2) * 2 + flip(core, offset % 2)
        )

    def stack(offset):
        return flip(z_high, offset // 2) * 2 + flip(z_low, offset % 2)

    used = [0]
    sent = []

    def remote(source, target, to, start=True):
        index = used[0]
        used[0] += 1
        copy = pltpu.make_async_remote_copy(
            src_ref=source,
            dst_ref=target,
            send_sem=send_sem.at[index],
            recv_sem=recv_sem.at[index],
            device_id=to,
            device_id_type=MESH,
        )
        copy.start()
        sent.append(copy)
        return copy

    def arrival(source, target, copy_index, to):
        return pltpu.make_async_remote_copy(
            src_ref=source,
            dst_ref=target,
            send_sem=send_sem.at[copy_index],
            recv_sem=recv_sem.at[copy_index],
            device_id=to,
            device_id_type=MESH,
        )

    def peer(offset):
        return {"dp": plane(offset), "tensor": z}

    def over(offset):
        return {"dp": dp, "tensor": stack(offset)}

    codes_copy = pltpu.make_async_copy(codes_hbm, codes, local_sem.at[0])
    pre_copy = pltpu.make_async_copy(pre_hbm, pre, local_sem.at[1])
    own_copy = pltpu.make_async_copy(grad_hbm, tokens.at[0], local_sem.at[2])
    codes_copy.start()
    pre_copy.start()
    own_copy.start()

    barrier = pltpu.get_barrier_semaphore()
    for offset in range(1, 8):
        pl.semaphore_signal(barrier, inc=1, device_id=peer(offset), device_id_type=MESH)
    for offset in range(1, 4):
        pl.semaphore_signal(barrier, inc=1, device_id=over(offset), device_id_type=MESH)
    pl.semaphore_wait(barrier, 10)

    lower, upper = pl.ds(0, half), pl.ds(half, half)
    from_x = [
        remote(grad_hbm.at[lower], tokens.at[1, lower], peer(2)),
    ]
    from_y = [
        remote(grad_hbm.at[upper], tokens.at[2, upper], peer(4)),
    ]

    depth = inputs_ref.shape[1]
    nt = (((1,), (1,)), ((), ()))
    tn = (((0,), (0,)), ((), ()))
    low_parts[0] = lax.dot_general(
        inputs_ref[...],
        first_ref[:, pl.ds(pl.multiple_of(z * depth, depth), depth)],
        nt,
        preferred_element_type=f32,
    ).astype(bf16)
    low_copies = [remote(low_parts.at[0], low_parts.at[r], over(r)) for r in range(1, 4)]

    own_rows = pl.ds(pl.multiple_of(dp * rows, rows), rows)
    adapter_rows[...] = jnp.transpose(first_ref[:, own_rows].astype(f32)).astype(bf16)
    scales = scales_ref[...]
    high = scales.astype(bf16).astype(f32)
    middle = (scales - high).astype(bf16).astype(f32)
    last = (scales - high) - middle
    pieces[...] = jnp.transpose(jnp.concatenate([high, middle, last], axis=0)).astype(bf16)
    codes_copy.wait()
    pre_copy.wait()
    own_copy.wait()

    def dequantize(step, carry):
        columns = pl.ds(pl.multiple_of(step * tile, tile), tile)
        shape = (scales_ref.shape[0], tile)
        place = lax.broadcasted_iota(jnp.int32, shape, 1) // block + step * (tile // block)
        chosen = jnp.where(lax.broadcasted_iota(jnp.int32, shape, 0) == place, 1.0, 0.0)
        spread = jnp.concatenate([chosen, chosen, chosen], axis=0).astype(bf16)
        expanded = jnp.dot(pieces[...], spread, preferred_element_type=f32)
        adapter = jnp.dot(adapter_rows[...], second_ref[:, columns], preferred_element_type=f32)
        merged = (
            (codes[:, columns].astype(f32) - 7.5) * expanded + adapter_scale_factor * adapter
        ).astype(bf16)
        weight[core * 2, :, columns] = merged[:group]
        weight[core * 2 + 1, :, columns] = merged[group:]
        merged_f = merged.astype(f32)
        stats[0, 0:1, columns] = jnp.sum(merged_f * merged_f, axis=0, keepdims=True)
        stats[0, 1:2, columns] = jnp.sum(
            tokens[0, :, columns].astype(f32) * pre[:, columns].astype(f32), axis=0, keepdims=True
        )
        return carry

    lax.fori_loop(0, steps // 2, dequantize, 0)
    from_x.append(remote(grad_hbm.at[upper], tokens.at[1, upper], peer(2)))
    from_y.append(remote(grad_hbm.at[lower], tokens.at[2, lower], peer(4)))
    lax.fori_loop(steps // 2, steps, dequantize, 0)

    stats_copies = [remote(stats.at[0], stats.at[o], peer(o)) for o in range(1, 8)]
    weight_index = used[0]
    own_half, other_half = pl.ds(core * 2, 2), pl.ds(2 - core * 2, 2)
    remote(weight.at[own_half], weight.at[own_half], peer(1))
    weight_arrival = arrival(
        weight.at[own_half], weight.at[other_half], weight_index, peer(1)
    )

    for copy in low_copies:
        copy.wait_recv()
    low[0] = (
        (low_parts[0].astype(f32) + low_parts[1].astype(f32))
        + (low_parts[2].astype(f32) + low_parts[3].astype(f32))
    ).astype(bf16)
    plane_low = [remote(low.at[0], low.at[b], peer(2 * b)) for b in range(1, 4)]

    for copy in stats_copies:
        copy.wait_recv()
    total = ((stats[0] + stats[1]) + (stats[2] + stats[3])) + (
        (stats[4] + stats[5]) + (stats[6] + stats[7])
    )
    norm = jnp.sqrt(total[0:1, :] + 1e-06)
    factor[...] = magnitude_ref[...].reshape(1, width) / norm
    magnitude_out[...] = (total[1:2, :] / norm).reshape(width)

    part = count // 4

    def part_rows(to_z):
        return pl.ds(pl.multiple_of(to_z * part, part), part)

    full = pl.ds(0, depth)
    groups = [pl.ds(n * group, group) for n in range(4)]

    def send_shares(which, columns):
        return [
            remote(
                product.at[which, part_rows(stack(r)), columns],
                shares.at[which, r, :, columns],
                over(r),
            )
            for r in range(1, 4)
        ]

    def sum_shares(which, copies, columns):
        for copy in copies:
            copy.wait_recv()
        target = returned if which == 0 else summed
        slot, to = which, peer(2 * which)
        if which in (1, 2):
            slot = 1 + z_high if which == 1 else 2 - z_high
            to_y, to_x = flip(y, slot - 1), flip(x, 2 - slot)
            to = {"dp": to_y * 4 + to_x * 2 + core, "tensor": z}
        target[which, :, columns] = (
            (product[which, part_rows(z), columns].astype(f32) + shares[which, 1, :, columns].astype(f32))
            + (shares[which, 2, :, columns].astype(f32) + shares[which, 3, :, columns].astype(f32))
        ).astype(bf16)
        if which == 0:
            return None
        return remote(
            summed.at[which, :, columns], returned.at[slot, :, columns], to
        )

    final_sends = []
    final_index = used[0]
    used[0] += 16

    def final_copy(which, tag, slot, n, target_rows, to):
        return pltpu.make_async_remote_copy(
            src_ref=returned.at[which, :, groups[n]],
            dst_ref=final.at[target_rows, groups[n]],
            send_sem=send_sem.at[final_index + tag * 4 + n],
            recv_sem=recv_sem.at[final_index + slot * 4 + n],
            device_id=to,
            device_id_type=MESH,
        )

    def send_final(tag, pieces_sent=range(4)):
        which, over_y, over_x = tag, tag // 2, tag % 2
        if tag in (1, 2):
            which = 1 + z_high if tag == 1 else 2 - z_high
            over_y, over_x = which - 1, 2 - which
        quarter_high, quarter_low = flip(y, over_y), flip(x, over_x)
        to_z = quarter_high * 2 + quarter_low
        slot = flip(quarter_high, z_high) * 2 + flip(quarter_low, z_low)
        for n in pieces_sent:
            copy = final_copy(which, tag, slot, n, part_rows(z), {"dp": dp, "tensor": to_z})

            @pl.when(to_z != z)
            def _(copy=copy):
                copy.start()

            @pl.when(to_z == z)
            def _(n=n):
                final[part_rows(z), groups[n]] = returned[which, :, groups[n]]

            final_sends.append((copy, to_z))

    def scale_tokens(lower_block, upper_block):
        def body(step, carry):
            columns = pl.ds(pl.multiple_of(step * tile, tile), tile)
            for which, part in ((lower_block, lower), (upper_block, upper)):
                scaled[part, columns] = (
                    tokens[which, part, columns].astype(f32) * factor[:, columns]
                ).astype(bf16)
            return carry

        lax.fori_loop(0, steps, body, 0)

    def multiply_group(which, n):
        columns = pl.ds(pl.multiple_of(n * group, group), group)
        product[which, :, columns] = lax.dot_general(
            scaled[...], weight[n], nt, preferred_element_type=f32
        ).astype(bf16)

    def second_product(which):
        if which == 0:
            back_acc[...] = jnp.zeros_like(back_acc)

        def body(step, carry):
            columns = pl.ds(pl.multiple_of(step * tile, tile), tile)
            values = (tokens[which, :, columns].astype(f32) * factor[:, columns]).astype(bf16)
            second_parts[which, :, columns] = lax.dot_general(
                low[which], values, tn, preferred_element_type=f32
            )
            if which == 0:
                back_acc[...] += lax.dot_general(
                    values, second_ref[:, columns], nt, preferred_element_type=f32
                )
            return carry

        lax.fori_loop(0, steps, body, 0)

    scale_tokens(0, 0)
    for n in range(2):
        multiply_group(0, core * 2 + n)
    from_x[0].wait_recv()
    far_lower = remote(tokens.at[1, lower], tokens.at[3, lower], peer(4))
    from_y[0].wait_recv()
    far_upper = remote(tokens.at[2, upper], tokens.at[3, upper], peer(2))

    weight_arrival.wait_recv()
    for n in range(2):
        multiply_group(0, 2 - core * 2 + n)
    shares_0 = send_shares(0, full)

    scale_tokens(1, 2)
    for n in range(4):
        multiply_group(1, n)
    shares_1 = send_shares(1, full)

    second_product(0)
    back_parts[0] = back_acc[...].astype(bf16)
    back_copies = [remote(back_parts.at[0], back_parts.at[r], over(r)) for r in range(1, 4)]
    sum_shares(0, shares_0, full)
    send_final(0)

    from_x[1].wait_recv()
    from_y[1].wait_recv()
    scale_tokens(2, 1)
    for n in range(4):
        multiply_group(2, n)
    shares_2 = send_shares(2, full)
    return_1 = sum_shares(1, shares_1, full)

    plane_low[0].wait_recv()
    second_product(1)
    plane_low[1].wait_recv()
    second_product(2)

    for copy in back_copies:
        copy.wait_recv()
    back = (
        (back_parts[0].astype(f32) + back_parts[1].astype(f32))
        + (back_parts[2].astype(f32) + back_parts[3].astype(f32))
    ).astype(bf16)
    slices = first_split.shape[0]
    piece = rank // slices
    gradient = adapter_scale_factor * lax.dot_general(
        back, inputs_ref[...], tn, preferred_element_type=f32
    )
    for index in range(slices):
        first_split[index] = gradient[index * piece : (index + 1) * piece, :]

    return_1.wait_recv()
    send_final(1)
    return_2 = sum_shares(2, shares_2, full)

    far_lower.wait_recv()
    far_upper.wait_recv()
    plane_low[2].wait_recv()
    scale_tokens(3, 3)
    shares_3 = []
    for n in range(4):
        multiply_group(3, n)
        shares_3.append(send_shares(3, groups[n]))
    return_2.wait_recv()
    send_final(2)
    returns_3 = [sum_shares(3, shares_3[n], groups[n]) for n in range(2)]
    second_product(3)
    returns_3 += [sum_shares(3, shares_3[n], groups[n]) for n in range(2, 4)]
    first_copies = [
        remote(first_split.at[plane(o)], first_recv.at[o], peer(o)) for o in range(1, 8)
    ]
    second_pair[0] = (second_parts[0] + second_parts[1]) + (second_parts[2] + second_parts[3])
    pair_copy = remote(second_pair.at[0], second_pair.at[1], peer(1))
    for n in range(4):
        returns_3[n].wait_recv()
        send_final(3, (n,))

    for copy in first_copies:
        copy.wait_recv()
    first_recv[0] = first_split[dp]
    first_full[dp] = (
        (first_recv[0] + first_recv[1]) + (first_recv[2] + first_recv[3])
    ) + ((first_recv[4] + first_recv[5]) + (first_recv[6] + first_recv[7]))
    first_index = used[0]
    for o in range(1, 8):
        remote(first_full.at[dp], first_full.at[dp], peer(o))

    pair_copy.wait_recv()
    second_out[...] = adapter_scale_factor * (second_pair[0] + second_pair[1])
    for o in range(1, 8):
        arrival(
            first_full.at[dp], first_full.at[plane(o)], first_index + o - 1, peer(o)
        ).wait_recv()
    first_out[...] = first_full[...].reshape(rank, depth)

    for n in range(4):
        for slot in range(1, 4):
            final_copy(slot, slot, slot, n, part_rows(stack(slot)), over(slot)).wait_recv()
    out_ref[...] = final[...]

    for copy in sent:
        copy.wait_send()
    for copy, to_z in final_sends:

        @pl.when(to_z != z)
        def _(copy=copy):
            copy.wait_send()


def on_device_fused(
    base_codes,
    block_scales,
    input_adapter_factor,
    output_adapter_factor,
    magnitude,
    inputs,
    grad_out,
    pre_scale,
):
    f32, bf16 = jnp.float32, jnp.bfloat16
    rows, width = base_codes.shape
    count, depth = inputs.shape
    rank = input_adapter_factor.shape[1]
    whole = pl.BlockSpec(memory_space=pltpu.VMEM)
    away = pl.BlockSpec(memory_space=pl.ANY)
    grad_inputs, first, second, grad_magnitude = pl.pallas_call(
        fused_kernel,
        out_shape=(
            jax.ShapeDtypeStruct((count, depth), bf16),
            jax.ShapeDtypeStruct((rank, depth), f32),
            jax.ShapeDtypeStruct((rank, width), f32),
            jax.ShapeDtypeStruct((width,), f32),
        ),
        in_specs=[away, whole, whole, whole, whole, whole, away, away],
        out_specs=(whole, whole, whole, whole),
        scratch_shapes=[
            pltpu.VMEM((rows, width), jnp.int32),
            pltpu.VMEM((count, width), bf16),
            pltpu.VMEM((4, count, width), bf16),
            pltpu.VMEM((4, rows // 2, width), bf16),
            pltpu.VMEM((8, 2, width), f32),
            pltpu.VMEM((1, width), f32),
            pltpu.VMEM((4, count, rank), bf16),
            pltpu.VMEM((4, count, rank), bf16),
            pltpu.VMEM((4, count, rank), bf16),
            pltpu.VMEM((count, rank), f32),
            pltpu.VMEM((count, width), bf16),
            pltpu.VMEM((4, count, depth), bf16),
            pltpu.VMEM((4, 4, count // 4, depth), bf16),
            pltpu.VMEM((4, count // 4, depth), bf16),
            pltpu.VMEM((4, count // 4, depth), bf16),
            pltpu.VMEM((count, depth), bf16),
            pltpu.VMEM((4, rank, width), f32),
            pltpu.VMEM((2, rank, width), f32),
            pltpu.VMEM((rows, 3 * block_scales.shape[1]), bf16),
            pltpu.VMEM((rows, rank), bf16),
            pltpu.VMEM((8, rank // 8, depth), f32),
            pltpu.VMEM((8, rank // 8, depth), f32),
            pltpu.VMEM((8, rank // 8, depth), f32),
            pltpu.SemaphoreType.DMA((3,)),
            pltpu.SemaphoreType.DMA((96,)),
            pltpu.SemaphoreType.DMA((96,)),
        ],
        compiler_params=pltpu.CompilerParams(
            collective_id=0, has_side_effects=True, vmem_limit_bytes=58 * 1024 * 1024
        ),
    )(
        base_codes,
        block_scales.T,
        input_adapter_factor.T,
        output_adapter_factor,
        magnitude,
        inputs,
        grad_out,
        pre_scale,
    )
    return grad_inputs, first.T, second, grad_magnitude


def solution(mesh):
    fits = mesh.shape["dp"] == 8 and mesh.shape["tensor"] == 4
    body = on_device_fused if fits else on_device
    in_specs = (
        P("dp", "tensor"),
        P("dp", "tensor"),
        P(),
        P(None, "tensor"),
        P("tensor"),
        P("dp", "tensor"),
        P("dp", "tensor"),
        P("dp", "tensor"),
    )
    out_specs = (P("dp", "tensor"), P("tensor", None), P(None, "tensor"), P("tensor"))
    return jax.shard_map(
        body, mesh=mesh, in_specs=in_specs, out_specs=out_specs, check_vma=False
    )
```
